256 devices in a mesh: section: 16 (over y, x_hi, core), fsdp: 16 (over z, x_lo).
Axes of the slice: x: 4 (x_hi: 2, x_lo: 2; x = x_hi * 2 + x_lo), y: 4, z: 8, core: 2. Of those that a mesh axis runs over, the one named last changes fastest.
Arguments:
- embeddings: bfloat16 [4, 1024, 2048], P(None, 'fsdp'), may hold values from -6 to 6
- section_weights: bfloat16 [16, 2048, 2048], P('section', 'fsdp'), may hold values from -0.125 to 0.125
- section_gains: bfloat16 [16, 2048], P('section', 'fsdp'), may hold values from 0.099609375 to 1.8984375
- top_direction: bfloat16 [4, 1024, 2048], P(None, 'fsdp'), may hold values from -6 to 6
- new_logprob: float32 [4, 1024], P(None, 'fsdp'), may hold values from -3 to -0.1
- old_logprob: float32 [4, 1024], P(None, 'fsdp'), may hold values from -3 to -0.1
- segment_ids: int32 [4, 1024], P(None, 'fsdp'), may hold values from 0 to 3, never falling along the last dimension, each value on 1 to 512 neighbouring positions
- advantages: float32 [4, 4], replicated, may hold values from -4 to 4
Outputs:
- weight_grad: float32 [16, 2048, 2048], P('section', 'fsdp')
- gain_grad: float32 [16, 2048], P('section', 'fsdp')
- gspo_loss: float32 [], replicated
The draws below stay inside these ranges and needn't reach their ends.
Inputs may be any that keep to these rules, and one draw needn't show every extreme that they name: `segment_ids`: in each micro-batch the numbers never fall along the tokens, every sequence 0 to 3 has 1 to 512 tokens, and one has exactly 512.
All inputs are finite; a program needn't handle non-finite values.
Results may differ from the reference program's by a relative error of at most 0.035.
Values may be sent and summed in bfloat16 or wider, within the bound.
No kernel may reach another device: no remote copies, remote signals or barrier semaphores. Data moves between devices by JAX's collectives and lax.ppermute only.
A program may use at most 64 MiB of HBM per device.

```python
import math
import jax
import jax.numpy as jnp
import numpy as np
from jax import lax

D = 2048
TOK_DEV = 64
MICRO = 4
SEGS = 4
MB_TOK = 1024
MOST = 512
LAYERS = 16
N_SECTION = 16
N_FSDP = 16


def steps_of(stream_key, shape, shards, least, high):
    loudness = 1.0
    for dim, blocks in shards:
        steps = jax.random.uniform(jax.random.fold_in(jax.random.fold_in(stream_key, 6), dim), (blocks,), jnp.float32, least / len(shards), high / len(shards))
        loudness = loudness * jnp.repeat(jnp.exp(steps), shape[dim] // blocks).reshape((-1,) + (1,) * (len(shape) - 1 - dim))
    return loudness


def split_up(count, total, most, skew):
    loads = [(1 << 20) // math.isqrt(standing ** skew) + 1 for standing in range(2, count + 1)]
    surplus, counts = total - most - (count - 1), [1] * (count - 1)
    while surplus > 0:
        movable = [i for i in range(count - 1) if counts[i] < most]
        whole, remaining = sum([loads[i] for i in movable]), surplus
        for i in movable:
            more = min(most - counts[i], max(1, remaining * loads[i] // whole), surplus)
            counts[i] = counts[i] + more
            surplus = surplus - more
    return np.array([most] + counts)


def ragged(rng, amount, total, limit, skew):
    if amount == 2:
        one = jax.random.randint(rng, (), max(1, total - limit), min(limit, total - 1) + 1)
        return jnp.stack([one, total - one])
    tallies = jnp.asarray(split_up(amount, total, limit, skew), jnp.int32)
    couples = (amount - 1) // 2
    donor, receiver = tallies[1:1 + 2 * couples:2], tallies[2:2 + 2 * couples:2]
    margin = jnp.minimum(donor - 1, limit - receiver)
    shifted = jax.random.randint(jax.random.fold_in(rng, 1), (couples,), 0, 1 << 20) % (margin + 1)
    tallies = tallies.at[1:1 + 2 * couples:2].set(donor - shifted).at[2:2 + 2 * couples:2].set(receiver + shifted)
    return tallies[jax.random.permutation(jax.random.fold_in(rng, 2), amount)]


def normal_values(key, shape, scale, reach, shards=(), kind=jnp.bfloat16):
    values = scale * jax.random.normal(key, shape, jnp.float32)
    if shards:
        values = values * steps_of(key, shape, shards, -0.22, 0.18)
    return jnp.clip(values, -reach, reach).astype(kind)


def setup_inputs(seed: int = 0) -> dict:
    key_of = jax.random.split(jax.random.key(seed), 9)
    return {
        "embeddings": normal_values(key_of[0], (MICRO, MB_TOK, D), 1.0, 6.0, ((1, 16),)),
        "section_weights": normal_values(key_of[1], (LAYERS, D, D), D ** -0.5, 0.125, ((0, 16), (1, 16))),
        "section_gains": jnp.clip(1.0 + 0.18 * jax.random.normal(key_of[2], (LAYERS, D), jnp.float32), 0.099609375, 1.8984375).astype(jnp.bfloat16),
        "top_direction": normal_values(key_of[3], (MICRO, MB_TOK, D), 1.0, 6.0, ((1, 16),)),
        "new_logprob": jnp.clip(-3.0 + 2.9 * jax.random.uniform(key_of[4], (MICRO, MB_TOK), jnp.float32) ** steps_of(key_of[4], (MICRO, MB_TOK), ((1, 16),), -0.2, 0.2), -3.0, -0.1),
        "old_logprob": jnp.clip(-3.0 + 2.9 * jax.random.uniform(key_of[5], (MICRO, MB_TOK), jnp.float32) ** steps_of(key_of[5], (MICRO, MB_TOK), ((1, 16),), -0.2, 0.2), -3.0, -0.1),
        "segment_ids": jax.vmap(lambda own: jnp.searchsorted(jnp.cumsum(ragged(own, SEGS, MB_TOK, MOST, 0)), jnp.arange(MB_TOK), side="right"))(jax.random.split(key_of[6], MICRO)).reshape((MICRO, MB_TOK)).astype(jnp.int32),
        "advantages": normal_values(key_of[7], (MICRO, SEGS), 1.0, 4.0, (), jnp.float32),
    }


clip_epsilon = 0.2
norm_epsilon = 1e-05

def layer_forward(states, matrix, gain_vec):
    widened = states.astype(jnp.float32)
    inverse_rms = lax.rsqrt(lax.optimization_barrier(jnp.mean(widened * widened, axis=-1, keepdims=True)) + norm_epsilon)
    normed = (widened * inverse_rms * gain_vec).astype(jnp.bfloat16)
    projected = jnp.dot(normed, matrix, preferred_element_type=jnp.float32)
    output = (widened + jax.nn.silu(projected)).astype(jnp.bfloat16)
    return (normed, projected, inverse_rms, output)

def layer_backward(upstream, states, projected, inverse_rms, matrix, gain_vec):
    sigmoid_pre = jax.nn.sigmoid(projected)
    upstream_f = upstream.astype(jnp.float32)
    pre_grad = (upstream_f * sigmoid_pre * (1.0 + projected * (1.0 - sigmoid_pre))).astype(jnp.bfloat16)
    norm_grad = lax.dot_general(pre_grad, matrix, (((1,), (1,)), ((), ())), preferred_element_type=jnp.float32)
    widened = states.astype(jnp.float32)
    scaled_grad = gain_vec * norm_grad
    input_grad = inverse_rms * scaled_grad - widened * inverse_rms ** 3 * lax.optimization_barrier(jnp.mean(scaled_grad * widened, axis=-1, keepdims=True))
    passed = (upstream_f + input_grad).astype(jnp.bfloat16)
    gain_rows = norm_grad * widened * inverse_rms
    return (pre_grad, passed, gain_rows)

def sequence_terms(new_logprob, old_logprob, segment_ids, advantages):
    labels = lax.broadcasted_iota(jnp.int32, (1, 1, SEGS), 2)
    member = (segment_ids[:, :, None] == labels).astype(jnp.float32)
    log_drift = new_logprob - old_logprob
    seq_sums = lax.optimization_barrier(jnp.sum(log_drift[:, :, None] * member, axis=1))
    seq_counts = lax.optimization_barrier(jnp.sum(member, axis=1))
    seq_ratio = jnp.exp(seq_sums / seq_counts)
    clipped = jnp.clip(seq_ratio, 1.0 - clip_epsilon, 1.0 + clip_epsilon)
    plain_term = seq_ratio * advantages
    bounded_term = clipped * advantages
    gspo_loss = -jnp.sum(jnp.minimum(plain_term, bounded_term))
    per_seq = jnp.where(plain_term <= bounded_term, -advantages * seq_ratio / seq_counts, 0.0)
    token_coef = lax.optimization_barrier(jnp.sum(member * per_seq[:, None, :], axis=2))
    return (gspo_loss, token_coef)

def rounded(value):
    return lax.optimization_barrier(value.astype(jnp.bfloat16)).astype(jnp.float32)

def reference(embeddings, section_weights, section_gains, top_direction, new_logprob, old_logprob, segment_ids, advantages):
    gspo_loss, token_coef = sequence_terms(new_logprob, old_logprob, segment_ids, advantages)
    states = embeddings.reshape(-1, D)
    kept = []
    for layer in range(N_SECTION):
        gain_vec = section_gains[layer].astype(jnp.float32)
        normed, projected, inverse_rms, output = layer_forward(states, section_weights[layer], gain_vec)
        kept.append((states, normed, projected, inverse_rms))
        states = output
    upstream = (token_coef[:, :, None] * top_direction.astype(jnp.float32)).astype(jnp.bfloat16).reshape(-1, D)
    weight_list = []
    gain_list = []
    for layer in range(N_SECTION - 1, -1, -1):
        layer_in, normed, projected, inverse_rms = kept[layer]
        gain_vec = section_gains[layer].astype(jnp.float32)
        pre_grad, upstream, gain_rows = layer_backward(upstream, layer_in, projected, inverse_rms, section_weights[layer], gain_vec)
        normed_parts = normed.reshape(MICRO, N_FSDP, TOK_DEV, D)
        grad_parts = pre_grad.reshape(MICRO, N_FSDP, TOK_DEV, D)
        gain_parts = gain_rows.reshape(MICRO, N_FSDP, TOK_DEV, D)
        weight_total = jnp.zeros((D, D), jnp.float32)
        gain_total = jnp.zeros((D,), jnp.float32)
        for shard in range(N_FSDP):
            left_rows = normed_parts[:, shard].reshape(-1, D)
            right_rows = grad_parts[:, shard].reshape(-1, D)
            partial_w = lax.dot_general(left_rows, right_rows, (((0,), (0,)), ((), ())), preferred_element_type=jnp.float32)
            weight_total = weight_total + rounded(partial_w)
            gain_total = gain_total + rounded(lax.optimization_barrier(jnp.sum(gain_parts[:, shard], axis=(0, 1))))
        weight_list.append(weight_total)
        gain_list.append(gain_total)
    weight_grad = jnp.stack(weight_list[::-1])
    gain_grad = jnp.stack(gain_list[::-1])
    return (weight_grad, gain_grad, gspo_loss)
```

```python
import functools

import jax
import jax.numpy as jnp
from jax import lax
from jax.experimental import pallas as pl
from jax.experimental.pallas import tpu as pltpu
from jax.sharding import PartitionSpec as P

clip_epsilon = 0.2
norm_epsilon = 1e-05
SPLIT = 1
BLOCK = 512
f32 = jnp.float32
bf16 = jnp.bfloat16


def vmem():
    return pl.BlockSpec(memory_space=pltpu.VMEM)


def params(mib):
    return pltpu.CompilerParams(vmem_limit_bytes=mib << 20)


def from_z_below(value):
    n = lax.axis_size("fsdp")
    return lax.ppermute(value, "fsdp", [(i, (i + 2) % n) for i in range(n)])


def from_z_above(value):
    n = lax.axis_size("fsdp")
    return lax.ppermute(value, "fsdp", [(i, (i - 2) % n) for i in range(n)])


def from_x(value):
    n = lax.axis_size("fsdp")
    return lax.ppermute(value, "fsdp", [(i, i ^ 1) for i in range(n)])


def from_partner(value, distance):
    n = lax.axis_size("fsdp")
    return lax.ppermute(value, "fsdp", [(i, i ^ distance) for i in range(n)])


GATHER = (
    ((0, 0), "zp", (-1, 0)),
    ((0, 0), "zm", (1, 0)),
    ((0, 0), "x", (0, 1)),
    ((-1, 0), "zp", (-2, 0)),
    ((1, 0), "zm", (2, 0)),
    ((-1, 0), "x", (-1, 1)),
    ((-2, 0), "zp", (-3, 0)),
    ((2, 0), "zm", (3, 0)),
    ((1, 0), "x", (1, 1)),
    ((-1, 1), "zp", (-2, 1)),
    ((1, 1), "zm", (2, 1)),
    ((-3, 0), "x", (-3, 1)),
    ((-3, 1), "zp", (-4, 1)),
    ((3, 0), "zm", (4, 0)),
    ((3, 0), "x", (3, 1)),
)
MOVE = {"zp": from_z_below, "zm": from_z_above, "x": from_x}
BACK = {"zp": from_z_above, "zm": from_z_below, "x": from_x}
KEYS = ((0, 0),) + tuple(entry[2] for entry in GATHER)


def shard_index(key):
    n = lax.axis_size("fsdp")
    me = lax.axis_index("fsdp")
    owner_z = lax.rem(me // 2 + key[0] + n // 2, n // 2)
    owner_a = lax.rem(lax.rem(me, 2) + key[1], 2)
    return owner_z * 2 + owner_a


def forward_kernel(tick, count, first, *refs):
    if first:
        fresh, matrix, gain, out, h_all, n_all, d_all, r_all, turned = refs
        incoming = None
    else:
        if tick < count:
            fresh, incoming, matrix, gain = refs[:4]
        else:
            incoming, matrix, gain = refs[:3]
        out, h_all, n_all, d_all, r_all, turned = refs[-6:]
    mine = lax.axis_index("section")
    slot = tick - mine
    live = (slot >= 0) & (slot < count)
    width = matrix.shape[0]

    def run(source, where):
        h = source[...].astype(f32)
        scale = lax.rsqrt(jnp.mean(h * h, axis=-1, keepdims=True) + norm_epsilon)
        n_all[where] = (h * scale * gain[...]).astype(bf16)
        h_all[where] = source[...]
        r_all[where] = jnp.broadcast_to(scale, r_all.shape[1:])
        for c in range(0, width, BLOCK):
            cols = slice(c, c + BLOCK)
            p = jnp.dot(n_all[where], matrix[:, cols], preferred_element_type=f32)
            gate = jax.nn.sigmoid(p)
            out[:, cols] = (source[:, cols].astype(f32) + p * gate).astype(bf16)
            d_all[where, :, cols] = gate * (1.0 + p * (1.0 - gate))

    if tick < count:
        @pl.when(mine == 0)
        def _():
            run(fresh.at[tick], tick)

    if not first:
        @pl.when(live & (mine > 0))
        def _():
            run(incoming, slot)

    idle = jnp.where(slot < 0, tick, tick - count)
    pieces = 8
    rows = width // pieces

    @pl.when(jnp.logical_not(live) & (idle < pieces))
    def _():
        at = pl.multiple_of(idle * rows, rows)
        for c in range(0, width, BLOCK):
            turned[c : c + BLOCK, pl.ds(at, rows)] = matrix[pl.ds(at, rows), c : c + BLOCK].T


def forward_tick(tick, count, fresh, incoming, matrix, gain, kept):
    rows, width = fresh.shape[1:]
    first = tick == 0
    operands = []
    if tick < count:
        operands.append(fresh)
    if not first:
        operands.append(incoming)
    operands += [matrix, gain]
    shapes = [
        jax.ShapeDtypeStruct((rows, width), bf16),
        jax.ShapeDtypeStruct((count, rows, width), bf16),
        jax.ShapeDtypeStruct((count, rows, width), bf16),
        jax.ShapeDtypeStruct((count, rows, width), f32),
        jax.ShapeDtypeStruct((count, rows, 128), f32),
        jax.ShapeDtypeStruct((width, width), bf16),
    ]
    aliases = {}
    if not first:
        aliases = {len(operands) + i: 1 + i for i in range(5)}
        operands += list(kept)
    results = pl.pallas_call(
        functools.partial(forward_kernel, tick, count, first),
        in_specs=[vmem()] * len(operands),
        out_specs=[vmem()] * 6,
        out_shape=shapes,
        input_output_aliases=aliases,
        compiler_params=params(24),
        name=f"forward_layer_{tick}",
    )(*operands)
    return results[0], tuple(results[1:])


def backward_kernel(tick, count, sections, first, *refs):
    if first:
        top, turned, gain, h_all, d_all, r_all, out, p_all, gain_sum, wide = refs
        incoming = None
    else:
        if tick < count:
            top, incoming, turned, gain, h_all, d_all, r_all = refs[:7]
        else:
            incoming, turned, gain, h_all, d_all, r_all = refs[:6]
        out, p_all, gain_sum, wide = refs[-4:]
    mine = lax.axis_index("section")
    slot = tick - (sections - 1 - mine)
    live = (slot >= 0) & (slot < count)
    width = turned.shape[0]

    def run(source, where):
        p_all[where] = (source[...].astype(f32) * d_all[where]).astype(bf16)
        scale = r_all[where][:, :1]
        dots = jnp.zeros((source.shape[0], 1), f32)
        for c in range(0, width, BLOCK):
            cols = slice(c, c + BLOCK)
            ng = jnp.dot(p_all[where], turned[:, cols], preferred_element_type=f32)
            h = h_all[where, :, cols].astype(f32)
            gain_rows = jnp.sum(ng * h * scale, axis=0, keepdims=True)
            gain_sum[:, cols] = jnp.where(where == 0, 0.0, gain_sum[:, cols]) + gain_rows
            scaled = gain[:, cols] * ng
            wide[:, cols] = scaled
            dots = dots + jnp.sum(scaled * h, axis=-1, keepdims=True)
        factor = scale * scale * scale * (dots / width)
        for c in range(0, width, BLOCK):
            cols = slice(c, c + BLOCK)
            h = h_all[where, :, cols].astype(f32)
            g = source[:, cols].astype(f32)
            out[:, cols] = (g + (scale * wide[:, cols] - h * factor)).astype(bf16)

    if tick < count:
        @pl.when(mine == sections - 1)
        def _():
            run(top.at[tick], tick)

    if not first:
        @pl.when(live & (mine < sections - 1))
        def _():
            run(incoming, slot)


def backward_tick(tick, count, sections, top, incoming, turned, gain, kept, grads):
    rows, width = top.shape[1:]
    first = tick == 0
    operands = []
    if tick < count:
        operands.append(top)
    if not first:
        operands.append(incoming)
    operands += [turned, gain, kept[0], kept[2], kept[3]]
    shapes = [
        jax.ShapeDtypeStruct((rows, width), bf16),
        jax.ShapeDtypeStruct((count, rows, width), bf16),
        jax.ShapeDtypeStruct((1, width), f32),
    ]
    aliases = {}
    if not first:
        aliases = {len(operands) + i: 1 + i for i in range(2)}
        operands += list(grads)
    results = pl.pallas_call(
        functools.partial(backward_kernel, tick, count, sections, first),
        in_specs=[vmem()] * len(operands),
        out_specs=[vmem()] * 3,
        out_shape=shapes,
        input_output_aliases=aliases,
        scratch_shapes=[pltpu.VMEM((rows, width), f32)],
        compiler_params=params(24),
        name=f"backward_layer_{tick}",
    )(*operands)
    return results[0], tuple(results[1:])


def weight_kernel(normed, grad, *outs):
    rows = outs[0].shape[0]
    width = grad.shape[1]
    for key, out in zip(KEYS, outs):
        at = pl.multiple_of(shard_index(key) * rows, rows)
        left = normed[:, pl.ds(at, rows)]
        for c in range(0, width, BLOCK):
            cols = slice(c, c + BLOCK)
            out[:, cols] = lax.dot_general(
                left, grad[:, cols], (((0,), (0,)), ((), ())), preferred_element_type=f32
            ).astype(bf16)


def weight_partials(normed, grad, shards):
    width = grad.shape[1]
    rows = width // shards
    return pl.pallas_call(
        weight_kernel,
        in_specs=[vmem(), vmem()],
        out_specs=[vmem()] * shards,
        out_shape=[jax.ShapeDtypeStruct((rows, width), bf16)] * shards,
        compiler_params=params(16),
        name="weight_partials",
    )(normed, grad)


def assemble_kernel(shards, *refs):
    pieces = refs[:shards]
    fresh, top, matrix, fresh_out, top_out, sems = refs[shards:]
    rows = pieces[0].shape[0]
    copies = [
        pltpu.make_async_copy(fresh, fresh_out, sems.at[shards]),
        pltpu.make_async_copy(top, top_out, sems.at[shards + 1]),
    ]
    for i, (key, piece) in enumerate(zip(KEYS, pieces)):
        at = pl.multiple_of(shard_index(key) * rows, rows)
        copies.append(pltpu.make_async_copy(piece, matrix.at[pl.ds(at, rows)], sems.at[i]))
    for copy in copies:
        copy.start()
    for copy in copies:
        copy.wait()


def assemble(pieces, fresh, top):
    shards = len(pieces)
    rows, width = pieces[0].shape
    return pl.pallas_call(
        functools.partial(assemble_kernel, shards),
        in_specs=[pl.BlockSpec(memory_space=pl.ANY)] * (shards + 2),
        out_specs=[vmem()] * 3,
        out_shape=[
            jax.ShapeDtypeStruct((shards * rows, width), bf16),
            jax.ShapeDtypeStruct(fresh.shape, bf16),
            jax.ShapeDtypeStruct(top.shape, bf16),
        ],
        scratch_shapes=[pltpu.SemaphoreType.DMA((shards + 2,))],
        compiler_params=params(12),
        name="assemble",
    )(*pieces, fresh, top)


def add_kernel(*refs):
    out = refs[-1]
    acc = refs[0][...].astype(f32)
    for ref in refs[1:-1]:
        acc = acc + ref[...].astype(f32)
    out[...] = acc.astype(out.dtype)


def add(*values, kind=None):
    return pl.pallas_call(
        add_kernel,
        in_specs=[vmem()] * len(values),
        out_specs=vmem(),
        out_shape=jax.ShapeDtypeStruct(values[0].shape, kind or values[0].dtype),
        compiler_params=params(8),
        name="add",
    )(*values)


def local(
    embeddings,
    section_weights,
    section_gains,
    top_direction,
    new_logprob,
    old_logprob,
    segment_ids,
    advantages,
):
    sections = lax.axis_size("section")
    shards = lax.axis_size("fsdp")
    shard = lax.axis_index("fsdp")
    micro_batches, row_count, width = embeddings.shape
    seq_count = advantages.shape[1]
    count = micro_batches * SPLIT
    rows = row_count // SPLIT
    share = width // shards

    labels = lax.broadcasted_iota(jnp.int32, (1, 1, seq_count), 2)
    member = (segment_ids[:, :, None] == labels).astype(f32)
    log_drift = new_logprob - old_logprob
    part_sums = jnp.sum(log_drift[:, :, None] * member, axis=1)
    part_counts = jnp.sum(member, axis=1)
    spread = jnp.zeros((1, width), f32)
    spread = lax.dynamic_update_slice(spread, section_gains.astype(f32), (0, shard * share))
    table = micro_batches * seq_count
    small = jnp.concatenate(
        [spread, part_sums.reshape(1, table), part_counts.reshape(1, table),
         jnp.zeros((1, 128 - 2 * table), f32)], axis=1
    )

    held = {(0, 0): section_weights[0]}
    distance = 1
    for i, (sent, move, got) in enumerate(GATHER):
        held[got] = MOVE[move](held[sent])
        if i % 3 == 2 and distance < shards:
            small = add(small, from_partner(small, distance))
            distance *= 2

    gain = small[:, :width]
    seq_sums = small[:, width : width + table].reshape(micro_batches, seq_count)
    seq_counts = small[:, width + table : width + 2 * table].reshape(micro_batches, seq_count)
    seq_ratio = jnp.exp(seq_sums / seq_counts)
    clipped = jnp.clip(seq_ratio, 1.0 - clip_epsilon, 1.0 + clip_epsilon)
    plain_term = seq_ratio * advantages
    bounded_term = clipped * advantages
    gspo_loss = -jnp.sum(jnp.minimum(plain_term, bounded_term))
    per_seq = jnp.where(plain_term <= bounded_term, -advantages * seq_ratio / seq_counts, 0.0)
    token_coef = jnp.sum(member * per_seq[:, None, :], axis=2)
    top_grad = (token_coef[:, :, None] * top_direction.astype(f32)).astype(bf16)
    top_grad = top_grad.reshape(count, rows, width)
    fresh = embeddings.reshape(count, rows, width)
    pieces = [held[key] for key in KEYS]
    pieces, fresh, top_grad, gain, gspo_loss = lax.optimization_barrier(
        (pieces, fresh, top_grad, gain, gspo_loss)
    )
    matrix, fresh, top_grad = assemble(pieces, fresh, top_grad)

    ticks = count + sections - 1
    state, kept = None, None
    for tick in range(ticks):
        state, kept = forward_tick(tick, count, fresh, state, matrix, gain, kept)
        route = [(s, s + 1) for s in range(sections - 1) if 0 <= tick - s < count]
        if route:
            state = lax.ppermute(state, "section", route)

    state, grads = None, None
    for tick in range(ticks):
        state, grads = backward_tick(
            tick, count, sections, top_grad, state, kept[4], gain, kept, grads
        )
        route = [
            (s, s - 1) for s in range(1, sections) if 0 <= tick - (sections - 1 - s) < count
        ]
        if route:
            state = lax.ppermute(state, "section", route)

    tokens = count * rows
    partials = weight_partials(
        kept[1].reshape(tokens, width), grads[0].reshape(tokens, width), shards
    )
    total = dict(zip(KEYS, partials))
    gain_total = add(grads[1], kind=bf16)
    distance = 1
    back = tuple(reversed(GATHER))
    for step in range(0, len(back), 3):
        came = {}
        for home, move, far in back[step : step + 3]:
            came.setdefault(home, []).append(BACK[move](total.pop(far)))
        if distance < shards:
            gain_total = add(gain_total, from_partner(gain_total, distance), kind=f32)
            distance *= 2
        for home, values in came.items():
            total[home] = add(total[home], *values, kind=f32 if home == (0, 0) else bf16)
    gain_share = lax.dynamic_slice(gain_total, (0, shard * share), (1, share))
    return (total[0, 0][None], gain_share, gspo_loss)


def solution(mesh):
    placed = (
        P(None, "fsdp", None),
        P("section", "fsdp", None),
        P("section", "fsdp"),
        P(None, "fsdp", None),
        P(None, "fsdp"),
        P(None, "fsdp"),
        P(None, "fsdp"),
        P(),
    )
    return jax.shard_map(
        local,
        mesh=mesh,
        in_specs=placed,
        out_specs=(P("section", "fsdp", None), P("section", "fsdp"), P()),
        check_vma=False,
    )
```

```python
import functools

import jax
import jax.numpy as jnp
from jax import lax
from jax.experimental import pallas as pl
from jax.experimental.pallas import tpu as pltpu
from jax.sharding import PartitionSpec as P

clip_epsilon = 0.2
norm_epsilon = 1e-05
SPLIT = 1
BLOCK = 512
f32 = jnp.float32
bf16 = jnp.bfloat16


def vmem():
    return pl.BlockSpec(memory_space=pltpu.VMEM)


def params(mib):
    return pltpu.CompilerParams(vmem_limit_bytes=mib << 20)


def from_z_below(value):
    n = lax.axis_size("fsdp")
    return lax.ppermute(value, "fsdp", [(i, (i + 2) % n) for i in range(n)])


def from_z_above(value):
    n = lax.axis_size("fsdp")
    return lax.ppermute(value, "fsdp", [(i, (i - 2) % n) for i in range(n)])


def from_x(value):
    n = lax.axis_size("fsdp")
    return lax.ppermute(value, "fsdp", [(i, i ^ 1) for i in range(n)])


def from_partner(value, distance):
    n = lax.axis_size("fsdp")
    return lax.ppermute(value, "fsdp", [(i, i ^ distance) for i in range(n)])


def crossed(section, sections):
    return (section // 2) % 2 if section < sections - 1 else 0


def hop(value, first, last, step):
    sections, n = lax.axis_size("section"), lax.axis_size("fsdp")
    route = []
    for s in range(max(first, 0), min(last, sections - 1) + 1):
        t = s + step
        if 0 <= t < sections:
            flip = crossed(s, sections) ^ crossed(t, sections)
            route += [(s * n + f, t * n + (f ^ flip)) for f in range(n)]
    return lax.ppermute(value, ("section", "fsdp"), route) if route else value


GATHER = (
    ((0, 0), "zp", (-1, 0)),
    ((0, 0), "zm", (1, 0)),
    ((0, 0), "x", (0, 1)),
    ((-1, 0), "zp", (-2, 0)),
    ((1, 0), "zm", (2, 0)),
    ((-1, 0), "x", (-1, 1)),
    ((-2, 0), "zp", (-3, 0)),
    ((2, 0), "zm", (3, 0)),
    ((1, 0), "x", (1, 1)),
    ((-1, 1), "zp", (-2, 1)),
    ((1, 1), "zm", (2, 1)),
    ((-3, 0), "x", (-3, 1)),
    ((-3, 1), "zp", (-4, 1)),
    ((3, 0), "zm", (4, 0)),
    ((3, 0), "x", (3, 1)),
)
MOVE = {"zp": from_z_below, "zm": from_z_above, "x": from_x}
BACK = {"zp": from_z_above, "zm": from_z_below, "x": from_x}
KEYS = ((0, 0),) + tuple(entry[2] for entry in GATHER)


def shard_index(key):
    n = lax.axis_size("fsdp")
    me = lax.axis_index("fsdp")
    owner_z = lax.rem(me // 2 + key[0] + n // 2, n // 2)
    owner_a = lax.rem(lax.rem(me, 2) + key[1], 2)
    return owner_z * 2 + owner_a


def forward_kernel(tick, count, first, *refs):
    if first:
        fresh, matrix, gain, out, h_all, n_all, d_all, r_all, turned = refs
        incoming = None
    else:
        if tick < count:
            fresh, incoming, matrix, gain = refs[:4]
        else:
            incoming, matrix, gain = refs[:3]
        out, h_all, n_all, d_all, r_all, turned = refs[-6:]
    mine = lax.axis_index("section")
    slot = tick - mine
    live = (slot >= 0) & (slot < count)
    width = matrix.shape[0]

    def run(source, where):
        h = source[...].astype(f32)
        scale = lax.rsqrt(jnp.mean(h * h, axis=-1, keepdims=True) + norm_epsilon)
        n_all[where] = (h * scale * gain[...]).astype(bf16)
        h_all[where] = source[...]
        r_all[where] = jnp.broadcast_to(scale, r_all.shape[1:])
        for c in range(0, width, BLOCK):
            cols = slice(c, c + BLOCK)
            p = jnp.dot(n_all[where], matrix[:, cols], preferred_element_type=f32)
            gate = jax.nn.sigmoid(p)
            out[:, cols] = (source[:, cols].astype(f32) + p * gate).astype(bf16)
            d_all[where, :, cols] = gate * (1.0 + p * (1.0 - gate))

    if tick < count:
        @pl.when(mine == 0)
        def _():
            run(fresh.at[tick], tick)

    if not first:
        @pl.when(live & (mine > 0))
        def _():
            run(incoming, slot)

    idle = jnp.where(slot < 0, tick, tick - count)
    pieces = 8
    rows = width // pieces

    @pl.when(jnp.logical_not(live) & (idle < pieces))
    def _():
        at = pl.multiple_of(idle * rows, rows)
        for c in range(0, width, BLOCK):
            turned[c : c + BLOCK, pl.ds(at, rows)] = matrix[pl.ds(at, rows), c : c + BLOCK].T


def forward_tick(tick, count, fresh, incoming, matrix, gain, kept):
    rows, width = fresh.shape[1:]
    first = tick == 0
    operands = []
    if tick < count:
        operands.append(fresh)
    if not first:
        operands.append(incoming)
    operands += [matrix, gain]
    shapes = [
        jax.ShapeDtypeStruct((rows, width), bf16),
        jax.ShapeDtypeStruct((count, rows, width), bf16),
        jax.ShapeDtypeStruct((count, rows, width), bf16),
        jax.ShapeDtypeStruct((count, rows, width), f32),
        jax.ShapeDtypeStruct((count, rows, 128), f32),
        jax.ShapeDtypeStruct((width, width), bf16),
    ]
    aliases = {}
    if not first:
        aliases = {len(operands) + i: 1 + i for i in range(5)}
        operands += list(kept)
    results = pl.pallas_call(
        functools.partial(forward_kernel, tick, count, first),
        in_specs=[vmem()] * len(operands),
        out_specs=[vmem()] * 6,
        out_shape=shapes,
        input_output_aliases=aliases,
        compiler_params=params(24),
        name=f"forward_layer_{tick}",
    )(*operands)
    return results[0], tuple(results[1:])


def backward_kernel(tick, count, sections, first, *refs):
    if first:
        top, turned, gain, h_all, d_all, r_all, out, p_all, gain_sum, wide = refs
        incoming = None
    else:
        if tick < count:
            top, incoming, turned, gain, h_all, d_all, r_all = refs[:7]
        else:
            incoming, turned, gain, h_all, d_all, r_all = refs[:6]
        out, p_all, gain_sum, wide = refs[-4:]
    mine = lax.axis_index("section")
    slot = tick - (sections - 1 - mine)
    live = (slot >= 0) & (slot < count)
    width = turned.shape[0]

    def run(source, where):
        p_all[where] = (source[...].astype(f32) * d_all[where]).astype(bf16)
        scale = r_all[where][:, :1]
        dots = jnp.zeros((source.shape[0], 1), f32)
        for c in range(0, width, BLOCK):
            cols = slice(c, c + BLOCK)
            ng = jnp.dot(p_all[where], turned[:, cols], preferred_element_type=f32)
            h = h_all[where, :, cols].astype(f32)
            gain_rows = jnp.sum(ng * h * scale, axis=0, keepdims=True)
            gain_sum[:, cols] = jnp.where(where == 0, 0.0, gain_sum[:, cols]) + gain_rows
            scaled = gain[:, cols] * ng
            wide[:, cols] = scaled
            dots = dots + jnp.sum(scaled * h, axis=-1, keepdims=True)
        factor = scale * scale * scale * (dots / width)
        for c in range(0, width, BLOCK):
            cols = slice(c, c + BLOCK)
            h = h_all[where, :, cols].astype(f32)
            g = source[:, cols].astype(f32)
            out[:, cols] = (g + (scale * wide[:, cols] - h * factor)).astype(bf16)

    if tick < count:
        @pl.when(mine == sections - 1)
        def _():
            run(top.at[tick], tick)

    if not first:
        @pl.when(live & (mine < sections - 1))
        def _():
            run(incoming, slot)


def backward_tick(tick, count, sections, top, incoming, turned, gain, kept, grads):
    rows, width = top.shape[1:]
    first = tick == 0
    operands = []
    if tick < count:
        operands.append(top)
    if not first:
        operands.append(incoming)
    operands += [turned, gain, kept[0], kept[2], kept[3]]
    shapes = [
        jax.ShapeDtypeStruct((rows, width), bf16),
        jax.ShapeDtypeStruct((count, rows, width), bf16),
        jax.ShapeDtypeStruct((1, width), f32),
    ]
    aliases = {}
    if not first:
        aliases = {len(operands) + i: 1 + i for i in range(2)}
        operands += list(grads)
    results = pl.pallas_call(
        functools.partial(backward_kernel, tick, count, sections, first),
        in_specs=[vmem()] * len(operands),
        out_specs=[vmem()] * 3,
        out_shape=shapes,
        input_output_aliases=aliases,
        scratch_shapes=[pltpu.VMEM((rows, width), f32)],
        compiler_params=params(24),
        name=f"backward_layer_{tick}",
    )(*operands)
    return results[0], tuple(results[1:])


def weight_kernel(normed, grad, *outs):
    rows = outs[0].shape[0]
    width = grad.shape[1]
    for key, out in zip(KEYS, outs):
        at = pl.multiple_of(shard_index(key) * rows, rows)
        left = normed[:, pl.ds(at, rows)]
        for c in range(0, width, BLOCK):
            cols = slice(c, c + BLOCK)
            out[:, cols] = lax.dot_general(
                left, grad[:, cols], (((0,), (0,)), ((), ())), preferred_element_type=f32
            ).astype(bf16)


def weight_partials(normed, grad, shards):
    width = grad.shape[1]
    rows = width // shards
    return pl.pallas_call(
        weight_kernel,
        in_specs=[vmem(), vmem()],
        out_specs=[vmem()] * shards,
        out_shape=[jax.ShapeDtypeStruct((rows, width), bf16)] * shards,
        compiler_params=params(16),
        name="weight_partials",
    )(normed, grad)


def assemble_kernel(shards, *refs):
    pieces = refs[:shards]
    fresh, top, matrix, fresh_out, top_out, sems = refs[shards:]
    rows = pieces[0].shape[0]
    copies = [
        pltpu.make_async_copy(fresh, fresh_out, sems.at[shards]),
        pltpu.make_async_copy(top, top_out, sems.at[shards + 1]),
    ]
    for i, (key, piece) in enumerate(zip(KEYS, pieces)):
        at = pl.multiple_of(shard_index(key) * rows, rows)
        copies.append(pltpu.make_async_copy(piece, matrix.at[pl.ds(at, rows)], sems.at[i]))
    for copy in copies:
        copy.start()
    for copy in copies:
        copy.wait()


def assemble(pieces, fresh, top):
    shards = len(pieces)
    rows, width = pieces[0].shape
    return pl.pallas_call(
        functools.partial(assemble_kernel, shards),
        in_specs=[pl.BlockSpec(memory_space=pl.ANY)] * (shards + 2),
        out_specs=[vmem()] * 3,
        out_shape=[
            jax.ShapeDtypeStruct((shards * rows, width), bf16),
            jax.ShapeDtypeStruct(fresh.shape, bf16),
            jax.ShapeDtypeStruct(top.shape, bf16),
        ],
        scratch_shapes=[pltpu.SemaphoreType.DMA((shards + 2,))],
        compiler_params=params(12),
        name="assemble",
    )(*pieces, fresh, top)


def small_kernel(seq_count, gains, new, old, ids, out):
    me = lax.axis_index("fsdp")
    share = gains.shape[1]
    micro_batches = new.shape[0]
    out[...] = jnp.zeros_like(out)
    row = lax.broadcasted_iota(jnp.int32, (out.shape[0], share), 0)
    wide = jnp.where(row == me // 2, gains[...].astype(f32), 0.0)
    out[:, :share] = jnp.where(me % 2 == 0, wide, 0.0)
    out[:, share : 2 * share] = jnp.where(me % 2 == 1, wide, 0.0)
    drift = new[...] - old[...]
    lane = lax.broadcasted_iota(jnp.int32, (micro_batches, 128), 1)
    sums = jnp.zeros((micro_batches, 128), f32)
    counts = jnp.zeros((micro_batches, 128), f32)
    for k in range(seq_count):
        member = ids[...] == k
        total = jnp.sum(jnp.where(member, drift, 0.0), axis=1, keepdims=True)
        number = jnp.sum(jnp.where(member, 1.0, 0.0), axis=1, keepdims=True)
        sums = jnp.where(lane == k, total, sums)
        counts = jnp.where(lane == k, number, counts)
    out[:micro_batches, 2 * share :] = sums
    out[micro_batches : 2 * micro_batches, 2 * share :] = counts


def small_part(gains, new, old, ids, seq_count, shards):
    share = gains.shape[1]
    return pl.pallas_call(
        functools.partial(small_kernel, seq_count),
        in_specs=[vmem()] * 4,
        out_specs=vmem(),
        out_shape=jax.ShapeDtypeStruct((shards // 2, 2 * share + 128), f32),
        compiler_params=params(8),
        name="small_part",
    )(gains, new, old, ids)


def coef_kernel(small, advantages, ids, direction, gain, loss, top):
    micro_batches, seq_count = advantages.shape
    pair = small.shape[1] - 128
    for r in range(small.shape[0]):
        gain[:, r * pair : (r + 1) * pair] = small[r : r + 1, :pair]
    sums = small[:micro_batches, pair : pair + seq_count]
    counts = small[micro_batches : 2 * micro_batches, pair : pair + seq_count]
    adv = advantages[...]
    ratio = jnp.exp(sums / counts)
    bounded = jnp.clip(ratio, 1.0 - clip_epsilon, 1.0 + clip_epsilon) * adv
    plain = ratio * adv
    least = jnp.sum(jnp.minimum(plain, bounded), axis=1, keepdims=True)
    loss[...] = -jnp.sum(least, axis=0, keepdims=True)
    per_seq = jnp.where(plain <= bounded, -adv * ratio / counts, 0.0)
    labels = ids[...]
    coef = jnp.zeros(labels.shape, f32)
    for k in range(seq_count):
        coef = coef + jnp.where(labels == k, per_seq[:, k : k + 1], 0.0)
    n = labels.shape[1]
    same = lax.broadcasted_iota(jnp.int32, (n, n), 0) == lax.broadcasted_iota(jnp.int32, (n, n), 1)
    for m in range(micro_batches):
        column = jnp.sum(jnp.where(same, coef[m : m + 1], 0.0), axis=1, keepdims=True)
        top[m] = (column * direction[m].astype(f32)).astype(bf16)


def coefficients(small, advantages, ids, direction):
    width = direction.shape[-1]
    return pl.pallas_call(
        coef_kernel,
        in_specs=[vmem()] * 4,
        out_specs=[vmem()] * 3,
        out_shape=[
            jax.ShapeDtypeStruct((1, width), f32),
            jax.ShapeDtypeStruct((1, 1), f32),
            jax.ShapeDtypeStruct(direction.shape, bf16),
        ],
        compiler_params=params(8),
        name="coefficients",
    )(small, advantages, ids, direction)


def add_kernel(*refs):
    out = refs[-1]
    acc = refs[0][...].astype(f32)
    for ref in refs[1:-1]:
        acc = acc + ref[...].astype(f32)
    out[...] = acc.astype(out.dtype)


def add(*values, kind=None):
    return pl.pallas_call(
        add_kernel,
        in_specs=[vmem()] * len(values),
        out_specs=vmem(),
        out_shape=jax.ShapeDtypeStruct(values[0].shape, kind or values[0].dtype),
        compiler_params=params(8),
        name="add",
    )(*values)


def local(
    embeddings,
    section_weights,
    section_gains,
    top_direction,
    new_logprob,
    old_logprob,
    segment_ids,
    advantages,
):
    sections = lax.axis_size("section")
    shards = lax.axis_size("fsdp")
    shard = lax.axis_index("fsdp")
    micro_batches, row_count, width = embeddings.shape
    seq_count = advantages.shape[1]
    count = micro_batches * SPLIT
    rows = row_count // SPLIT
    share = width // shards

    small = small_part(section_gains, new_logprob, old_logprob, segment_ids, seq_count, shards)

    held = {(0, 0): section_weights[0]}
    distance = 1
    for step in range(0, len(GATHER), 3):
        came = [MOVE[move](held[sent]) for sent, move, _ in GATHER[step : step + 3]]
        if distance < shards:
            small = add(small, from_partner(small, distance))
            distance *= 2
        came, small = lax.optimization_barrier((came, small))
        held.update(zip([entry[2] for entry in GATHER[step : step + 3]], came))

    gain, gspo_loss, top_grad = coefficients(small, advantages, segment_ids, top_direction)
    top_grad = top_grad.reshape(count, rows, width)
    fresh = embeddings.reshape(count, rows, width)
    pieces = [held[key] for key in KEYS]
    pieces, fresh, top_grad, gain = lax.optimization_barrier((pieces, fresh, top_grad, gain))
    matrix, fresh, top_grad = assemble(pieces, fresh, top_grad)

    ticks = count + sections - 1
    state, kept = None, None
    for tick in range(ticks):
        state, kept = forward_tick(tick, count, fresh, state, matrix, gain, kept)
        even = tick - tick % 2
        if tick < ticks - 1:
            state = hop(state, even + 1 - count, even + 1, 1)

    state, grads = None, None
    for tick in range(ticks):
        state, grads = backward_tick(
            tick, count, sections, top_grad, state, kept[4], gain, kept, grads
        )
        even = tick - tick % 2
        if tick < ticks - 1:
            state = hop(state, sections - 2 - even, sections - 2 - even + count, -1)

    tokens = count * rows
    partials = weight_partials(
        kept[1].reshape(tokens, width), grads[0].reshape(tokens, width), shards
    )
    total = dict(zip(KEYS, partials))
    gain_total = add(grads[1], kind=bf16)
    distance = 1
    back = tuple(reversed(GATHER))
    for step in range(0, len(back), 3):
        came = {}
        for home, move, far in back[step : step + 3]:
            came.setdefault(home, []).append(BACK[move](total.pop(far)))
        if distance < shards:
            gain_total = add(gain_total, from_partner(gain_total, distance), kind=f32)
            distance *= 2
        came, gain_total = lax.optimization_barrier((came, gain_total))
        for home, values in came.items():
            total[home] = add(total[home], *values, kind=f32 if home == (0, 0) else bf16)
    gain_share = lax.dynamic_slice(gain_total, (0, shard * share), (1, share))
    return (total[0, 0][None], gain_share, gspo_loss[0, 0])


def solution(mesh):
    placed = (
        P(None, "fsdp", None),
        P("section", "fsdp", None),
        P("section", "fsdp"),
        P(None, "fsdp", None),
        P(None, "fsdp"),
        P(None, "fsdp"),
        P(None, "fsdp"),
        P(),
    )
    return jax.shard_map(
        local,
        mesh=mesh,
        in_specs=placed,
        out_specs=(P("section", "fsdp", None), P("section", "fsdp"), P()),
        check_vma=False,
    )
```

```python
import functools

import jax
import jax.numpy as jnp
from jax import lax
from jax.experimental import pallas as pl
from jax.experimental.pallas import tpu as pltpu
from jax.sharding import PartitionSpec as P

clip_epsilon = 0.2
norm_epsilon = 1e-05
SPLIT = 2
SKEW = 2
GROUP = 8
TOP_TICK = 12
BLOCK = 512
f32 = jnp.float32
bf16 = jnp.bfloat16


def vmem():
    return pl.BlockSpec(memory_space=pltpu.VMEM)


def params(mib):
    return pltpu.CompilerParams(vmem_limit_bytes=mib << 20)


def from_z_below(value):
    n = lax.axis_size("fsdp")
    return lax.ppermute(value, "fsdp", [(i, (i + 2) % n) for i in range(n)])


def from_z_above(value):
    n = lax.axis_size("fsdp")
    return lax.ppermute(value, "fsdp", [(i, (i - 2) % n) for i in range(n)])


def from_x(value):
    n = lax.axis_size("fsdp")
    return lax.ppermute(value, "fsdp", [(i, i ^ 1) for i in range(n)])


def from_partner(value, distance):
    n = lax.axis_size("fsdp")
    return lax.ppermute(value, "fsdp", [(i, i ^ distance) for i in range(n)])


def crossed(section, sections):
    return (section // 2) % 2 if section < sections - 1 else 0


def hop(value, tick, count, step):
    sections, n = lax.axis_size("section"), lax.axis_size("fsdp")
    ticks = range(tick - tick % GROUP, tick - tick % GROUP + GROUP)
    route = []
    for s in range(sections):
        place = s if step > 0 else sections - 1 - s
        t = s + step
        if 0 <= t < sections and any(0 <= k - SKEW * place < count for k in ticks):
            flip = crossed(s, sections) ^ crossed(t, sections)
            route += [(s * n + f, t * n + (f ^ flip)) for f in range(n)]
    return lax.ppermute(value, ("section", "fsdp"), route)


GATHER = (
    ((0, 0), "zp", (-1, 0)),
    ((0, 0), "zm", (1, 0)),
    ((0, 0), "x", (0, 1)),
    ((-1, 0), "zp", (-2, 0)),
    ((1, 0), "zm", (2, 0)),
    ((-1, 0), "x", (-1, 1)),
    ((-2, 0), "zp", (-3, 0)),
    ((2, 0), "zm", (3, 0)),
    ((1, 0), "x", (1, 1)),
    ((-1, 1), "zp", (-2, 1)),
    ((1, 1), "zm", (2, 1)),
    ((-3, 0), "x", (-3, 1)),
    ((-3, 1), "zp", (-4, 1)),
    ((3, 0), "zm", (4, 0)),
    ((3, 0), "x", (3, 1)),
)
MOVE = {"zp": from_z_below, "zm": from_z_above, "x": from_x}
BACK = {"zp": from_z_above, "zm": from_z_below, "x": from_x}
KEYS = ((0, 0),) + tuple(entry[2] for entry in GATHER)


def shard_index(key):
    n = lax.axis_size("fsdp")
    me = lax.axis_index("fsdp")
    owner_z = lax.rem(me // 2 + key[0] + n // 2, n // 2)
    owner_a = lax.rem(lax.rem(me, 2) + key[1], 2)
    return owner_z * 2 + owner_a


def forward_kernel(tick, count, *refs):
    refs = list(refs)
    fresh = refs.pop(0) if tick < count else None
    incoming = refs.pop(0) if tick >= SKEW else None
    matrix, gain = refs[:2]
    out, h_all, n_all, d_all, r_all, turned = refs[-6:]
    mine = lax.axis_index("section")
    slot = tick - SKEW * mine
    live = (slot >= 0) & (slot < count)
    width = matrix.shape[0]

    def run(source, where):
        h = source[...].astype(f32)
        scale = lax.rsqrt(jnp.mean(h * h, axis=-1, keepdims=True) + norm_epsilon)
        n_all[where] = (h * scale * gain[...]).astype(bf16)
        h_all[where] = source[...]
        r_all[where] = jnp.broadcast_to(scale, r_all.shape[1:])
        for c in range(0, width, BLOCK):
            cols = slice(c, c + BLOCK)
            p = jnp.dot(n_all[where], matrix[:, cols], preferred_element_type=f32)
            gate = jax.nn.sigmoid(p)
            out[:, cols] = (source[:, cols].astype(f32) + p * gate).astype(bf16)
            d_all[where, :, cols] = gate * (1.0 + p * (1.0 - gate))

    if tick < count:
        @pl.when(mine == 0)
        def _():
            run(fresh.at[tick], tick)

    if incoming is not None:
        @pl.when(live & (mine > 0))
        def _():
            run(incoming, slot)

    idle = jnp.where(slot < 0, tick, tick - count)
    pieces = 8
    rows = width // pieces

    @pl.when(jnp.logical_not(live) & (idle < pieces))
    def _():
        at = pl.multiple_of(idle * rows, rows)
        for c in range(0, width, BLOCK):
            turned[c : c + BLOCK, pl.ds(at, rows)] = matrix[pl.ds(at, rows), c : c + BLOCK].T


def forward_tick(tick, count, fresh, incoming, matrix, gain, kept):
    rows, width = fresh.shape[1:]
    operands = []
    if tick < count:
        operands.append(fresh)
    if incoming is not None:
        operands.append(incoming)
    operands += [matrix, gain]
    first = tick == 0
    shapes = [
        jax.ShapeDtypeStruct((rows, width), bf16),
        jax.ShapeDtypeStruct((count, rows, width), bf16),
        jax.ShapeDtypeStruct((count, rows, width), bf16),
        jax.ShapeDtypeStruct((count, rows, width), f32),
        jax.ShapeDtypeStruct((count, rows, 128), f32),
        jax.ShapeDtypeStruct((width, width), bf16),
    ]
    aliases = {}
    if not first:
        aliases = {len(operands) + i: 1 + i for i in range(5)}
        operands += list(kept)
    results = pl.pallas_call(
        functools.partial(forward_kernel, tick, count),
        in_specs=[vmem()] * len(operands),
        out_specs=[vmem()] * 6,
        out_shape=shapes,
        input_output_aliases=aliases,
        compiler_params=params(24),
        name=f"forward_layer_{tick}",
    )(*operands)
    return results[0], tuple(results[1:])


def backward_kernel(tick, count, sections, *refs):
    refs = list(refs)
    top = refs.pop(0) if tick < count else None
    incoming = refs.pop(0) if tick >= SKEW else None
    turned, gain, h_all, d_all, r_all = refs[:5]
    out, p_all, gain_sum, wide = refs[-4:]
    mine = lax.axis_index("section")
    slot = tick - SKEW * (sections - 1 - mine)
    live = (slot >= 0) & (slot < count)
    width = turned.shape[0]

    def run(source, where):
        p_all[where] = (source[...].astype(f32) * d_all[where]).astype(bf16)
        scale = r_all[where][:, :1]
        dots = jnp.zeros((source.shape[0], 1), f32)
        for c in range(0, width, BLOCK):
            cols = slice(c, c + BLOCK)
            ng = jnp.dot(p_all[where], turned[:, cols], preferred_element_type=f32)
            h = h_all[where, :, cols].astype(f32)
            gain_rows = jnp.sum(ng * h * scale, axis=0, keepdims=True)
            gain_sum[:, cols] = jnp.where(where == 0, 0.0, gain_sum[:, cols]) + gain_rows
            scaled = gain[:, cols] * ng
            wide[:, cols] = scaled
            dots = dots + jnp.sum(scaled * h, axis=-1, keepdims=True)
        factor = scale * scale * scale * (dots / width)
        for c in range(0, width, BLOCK):
            cols = slice(c, c + BLOCK)
            h = h_all[where, :, cols].astype(f32)
            g = source[:, cols].astype(f32)
            out[:, cols] = (g + (scale * wide[:, cols] - h * factor)).astype(bf16)

    if tick < count:
        @pl.when(mine == sections - 1)
        def _():
            run(top.at[tick], tick)

    if incoming is not None:
        @pl.when(live & (mine < sections - 1))
        def _():
            run(incoming, slot)


def backward_tick(tick, count, sections, top, incoming, turned, gain, kept, grads):
    rows, width = top.shape[1:]
    first = tick == 0
    operands = []
    if tick < count:
        operands.append(top)
    if incoming is not None:
        operands.append(incoming)
    operands += [turned, gain, kept[0], kept[2], kept[3]]
    shapes = [
        jax.ShapeDtypeStruct((rows, width), bf16),
        jax.ShapeDtypeStruct((count, rows, width), bf16),
        jax.ShapeDtypeStruct((1, width), f32),
    ]
    aliases = {}
    if not first:
        aliases = {len(operands) + i: 1 + i for i in range(2)}
        operands += list(grads)
    results = pl.pallas_call(
        functools.partial(backward_kernel, tick, count, sections),
        in_specs=[vmem()] * len(operands),
        out_specs=[vmem()] * 3,
        out_shape=shapes,
        input_output_aliases=aliases,
        scratch_shapes=[pltpu.VMEM((rows, width), f32)],
        compiler_params=params(24),
        name=f"backward_layer_{tick}",
    )(*operands)
    return results[0], tuple(results[1:])


def weight_kernel(normed, grad, *outs):
    rows = outs[0].shape[0]
    width = grad.shape[1]
    for key, out in zip(KEYS, outs):
        at = pl.multiple_of(shard_index(key) * rows, rows)
        left = normed[:, pl.ds(at, rows)]
        for c in range(0, width, BLOCK):
            cols = slice(c, c + BLOCK)
            out[:, cols] = lax.dot_general(
                left, grad[:, cols], (((0,), (0,)), ((), ())), preferred_element_type=f32
            ).astype(bf16)


def weight_partials(normed, grad, shards):
    width = grad.shape[1]
    rows = width // shards
    return pl.pallas_call(
        weight_kernel,
        in_specs=[vmem(), vmem()],
        out_specs=[vmem()] * shards,
        out_shape=[jax.ShapeDtypeStruct((rows, width), bf16)] * shards,
        compiler_params=params(16),
        name="weight_partials",
    )(normed, grad)


def assemble_kernel(shards, *refs):
    pieces = refs[:shards]
    small, matrix, gain, sems = refs[shards:]
    rows = pieces[0].shape[0]
    copies = []
    for i, (key, piece) in enumerate(zip(KEYS, pieces)):
        at = pl.multiple_of(shard_index(key) * rows, rows)
        copies.append(pltpu.make_async_copy(piece, matrix.at[pl.ds(at, rows)], sems.at[i]))
    for copy in copies:
        copy.start()

    pair = small.shape[1] - 128
    for r in range(small.shape[0]):
        gain[:, r * pair : (r + 1) * pair] = small[r : r + 1, :pair]
    for copy in copies:
        copy.wait()


def assemble(pieces, small):
    shards = len(pieces)
    rows, width = pieces[0].shape
    return pl.pallas_call(
        functools.partial(assemble_kernel, shards),
        in_specs=[pl.BlockSpec(memory_space=pl.ANY)] * shards + [vmem()],
        out_specs=[vmem()] * 2,
        out_shape=[
            jax.ShapeDtypeStruct((shards * rows, width), bf16),
            jax.ShapeDtypeStruct((1, width), f32),
        ],
        scratch_shapes=[pltpu.SemaphoreType.DMA((shards,))],
        compiler_params=params(12),
        name="assemble",
    )(*pieces, small)


def small_kernel(seq_count, *refs):
    gains, new, old, ids, advantages, *arrays = refs[:8]
    out, ids_out, adv_out, *kept, sems = refs[8:]
    copies = [pltpu.make_async_copy(a, b, sems.at[i]) for i, (a, b) in enumerate(zip(arrays, kept))]
    for copy in copies:
        copy.start()
    ids_out[...] = ids[...]
    adv_out[...] = advantages[...]
    me = lax.axis_index("fsdp")
    share = gains.shape[1]
    micro_batches = new.shape[0]
    out[...] = jnp.zeros_like(out)
    row = lax.broadcasted_iota(jnp.int32, (out.shape[0], share), 0)
    wide = jnp.where(row == me // 2, gains[...].astype(f32), 0.0)
    out[:, :share] = jnp.where(me % 2 == 0, wide, 0.0)
    out[:, share : 2 * share] = jnp.where(me % 2 == 1, wide, 0.0)
    drift = new[...] - old[...]
    lane = lax.broadcasted_iota(jnp.int32, (micro_batches, 128), 1)
    sums = jnp.zeros((micro_batches, 128), f32)
    counts = jnp.zeros((micro_batches, 128), f32)
    for k in range(seq_count):
        member = ids[...] == k
        total = jnp.sum(jnp.where(member, drift, 0.0), axis=1, keepdims=True)
        number = jnp.sum(jnp.where(member, 1.0, 0.0), axis=1, keepdims=True)
        sums = jnp.where(lane == k, total, sums)
        counts = jnp.where(lane == k, number, counts)
    out[:micro_batches, 2 * share :] = sums
    out[micro_batches : 2 * micro_batches, 2 * share :] = counts
    for copy in copies:
        copy.wait()


def small_part(gains, new, old, ids, advantages, arrays, shards):
    share = gains.shape[1]
    return pl.pallas_call(
        functools.partial(small_kernel, advantages.shape[1]),
        in_specs=[vmem()] * 5 + [pl.BlockSpec(memory_space=pl.ANY)] * len(arrays),
        out_specs=[vmem()] * (3 + len(arrays)),
        out_shape=[
            jax.ShapeDtypeStruct((shards // 2, 2 * share + 128), f32),
            jax.ShapeDtypeStruct(ids.shape, ids.dtype),
            jax.ShapeDtypeStruct(advantages.shape, f32),
        ]
        + [jax.ShapeDtypeStruct(a.shape, a.dtype) for a in arrays],
        scratch_shapes=[pltpu.SemaphoreType.DMA((len(arrays),))],
        compiler_params=params(12),
        name="small_part",
    )(gains, new, old, ids, advantages, *arrays)


def top_kernel(small, advantages, ids, direction, loss, top):
    micro_batches, seq_count = advantages.shape
    pair = small.shape[1] - 128
    sums = small[:micro_batches, pair : pair + seq_count]
    counts = small[micro_batches : 2 * micro_batches, pair : pair + seq_count]
    adv = advantages[...]
    ratio = jnp.exp(sums / counts)
    bounded = jnp.clip(ratio, 1.0 - clip_epsilon, 1.0 + clip_epsilon) * adv
    plain = ratio * adv
    least = jnp.sum(jnp.minimum(plain, bounded), axis=1, keepdims=True)
    loss[...] = -jnp.sum(least, axis=0, keepdims=True)

    @pl.when(lax.axis_index("section") == lax.axis_size("section") - 1)
    def _():
        per_seq = jnp.where(plain <= bounded, -adv * ratio / counts, 0.0)
        labels = ids[...]
        coef = jnp.zeros(labels.shape, f32)
        for k in range(seq_count):
            coef = coef + jnp.where(labels == k, per_seq[:, k : k + 1], 0.0)
        n = labels.shape[1]
        rows = lax.broadcasted_iota(jnp.int32, (n, n), 0)
        same = rows == lax.broadcasted_iota(jnp.int32, (n, n), 1)
        size = top.shape[1]
        for m in range(micro_batches):
            column = jnp.sum(jnp.where(same, coef[m : m + 1], 0.0), axis=1, keepdims=True)
            for i in range(n // size):
                part = slice(i * size, (i + 1) * size)
                scaled = column[part] * direction[m, part].astype(f32)
                top[m * (n // size) + i] = scaled.astype(bf16)


def top_cotangent(small, advantages, ids, direction, count):
    micro_batches, rows, width = direction.shape
    return pl.pallas_call(
        top_kernel,
        in_specs=[vmem()] * 4,
        out_specs=[vmem()] * 2,
        out_shape=[
            jax.ShapeDtypeStruct((1, 1), f32),
            jax.ShapeDtypeStruct((count, micro_batches * rows // count, width), bf16),
        ],
        compiler_params=params(8),
        name="top_cotangent",
    )(small, advantages, ids, direction)


def add_kernel(*refs):
    out = refs[-1]
    acc = refs[0][...].astype(f32)
    for ref in refs[1:-1]:
        acc = acc + ref[...].astype(f32)
    out[...] = acc.astype(out.dtype)


def add(*values, kind=None):
    return pl.pallas_call(
        add_kernel,
        in_specs=[vmem()] * len(values),
        out_specs=vmem(),
        out_shape=jax.ShapeDtypeStruct(values[0].shape, kind or values[0].dtype),
        compiler_params=params(8),
        name="add",
    )(*values)


def local(
    embeddings,
    section_weights,
    section_gains,
    top_direction,
    new_logprob,
    old_logprob,
    segment_ids,
    advantages,
):
    sections = lax.axis_size("section")
    shards = lax.axis_size("fsdp")
    shard = lax.axis_index("fsdp")
    micro_batches, row_count, width = embeddings.shape
    seq_count = advantages.shape[1]
    count = micro_batches * SPLIT
    rows = row_count // SPLIT
    share = width // shards

    held = {(0, 0): section_weights[0]}
    small, ids, adv, fresh, direction, own = small_part(
        section_gains,
        new_logprob,
        old_logprob,
        segment_ids,
        advantages,
        (embeddings, top_direction, held[0, 0]),
        shards,
    )
    distance = 1
    for step in range(0, len(GATHER), 3):
        came = [MOVE[move](held[sent]) for sent, move, _ in GATHER[step : step + 3]]
        if distance < shards:
            other = from_partner(small, distance)
            came, other = lax.optimization_barrier((came, other))
            small = add(small, other)
            distance *= 2
        held.update(zip([entry[2] for entry in GATHER[step : step + 3]], came))
    fresh = fresh.reshape(count, rows, width)
    pieces = [own] + [held[key] for key in KEYS[1:]]
    matrix, gain = assemble(pieces, small)

    ticks = SKEW * (sections - 1) + count
    kept, moved = None, {}
    for tick in range(ticks):
        state, kept = forward_tick(
            tick, count, fresh, moved.pop(tick - SKEW, None), matrix, gain, kept
        )
        if tick < ticks - SKEW:
            moved[tick] = hop(state, tick, count, 1)
        if tick == TOP_TICK:
            small, kept = lax.optimization_barrier((small, kept))
            gspo_loss, top_grad = top_cotangent(small, adv, ids, direction, count)
            gspo_loss, top_grad, kept = lax.optimization_barrier((gspo_loss, top_grad, kept))

    grads, moved = None, {}
    for tick in range(ticks):
        state, grads = backward_tick(
            tick, count, sections, top_grad, moved.pop(tick - SKEW, None), kept[4], gain, kept, grads
        )
        if tick < ticks - SKEW:
            moved[tick] = hop(state, tick, count, -1)
    tokens = count * rows
    partials = weight_partials(
        kept[1].reshape(tokens, width), grads[0].reshape(tokens, width), shards
    )
    total = dict(zip(KEYS, partials))
    gain_total = add(grads[1], kind=bf16)
    distance = 1
    back = tuple(reversed(GATHER))
    for step in range(0, len(back), 3):
        came = {}
        for home, move, far in back[step : step + 3]:
            came.setdefault(home, []).append(BACK[move](total.pop(far)))
        if distance < shards:
            other = from_partner(gain_total, distance)
            came, other = lax.optimization_barrier((came, other))
            gain_total = add(gain_total, other, kind=f32)
            distance *= 2
        for home, values in came.items():
            total[home] = add(total[home], *values, kind=f32 if home == (0, 0) else bf16)
    gain_share = lax.dynamic_slice(gain_total, (0, shard * share), (1, share))
    return (total[0, 0][None], gain_share, gspo_loss[0, 0])


def solution(mesh):
    placed = (
        P(None, "fsdp", None),
        P("section", "fsdp", None),
        P("section", "fsdp"),
        P(None, "fsdp", None),
        P(None, "fsdp"),
        P(None, "fsdp"),
        P(None, "fsdp"),
        P(),
    )
    return jax.shard_map(
        local,
        mesh=mesh,
        in_specs=placed,
        out_specs=(P("section", "fsdp", None), P("section", "fsdp"), P()),
        check_vma=False,
    )
```

```python
import functools

import jax
import jax.numpy as jnp
from jax import lax
from jax.experimental import pallas as pl
from jax.experimental.pallas import tpu as pltpu
from jax.sharding import PartitionSpec as P

clip_epsilon = 0.2
norm_epsilon = 1e-05
COUNT = 4
SKEW = 2
GROUP = 8
TOP_TICK = 6
BLOCK = 512
f32 = jnp.float32
bf16 = jnp.bfloat16


def vmem():
    return pl.BlockSpec(memory_space=pltpu.VMEM)


def params(mib):
    return pltpu.CompilerParams(vmem_limit_bytes=mib << 20)


def from_z_below(value):
    n = lax.axis_size("fsdp")
    return lax.ppermute(value, "fsdp", [(i, (i + 2) % n) for i in range(n)])


def from_z_above(value):
    n = lax.axis_size("fsdp")
    return lax.ppermute(value, "fsdp", [(i, (i - 2) % n) for i in range(n)])


def from_x(value):
    n = lax.axis_size("fsdp")
    return lax.ppermute(value, "fsdp", [(i, i ^ 1) for i in range(n)])


def from_partner(value, distance):
    n = lax.axis_size("fsdp")
    return lax.ppermute(value, "fsdp", [(i, i ^ distance) for i in range(n)])


def from_core(value):
    n = lax.axis_size("section")
    return lax.ppermute(value, "section", [(i, i ^ 1) for i in range(n)])


def place():
    section = lax.axis_index("section")
    return section // 2, lax.rem(section, 2)


def crossed(stage, stages):
    return stage % 2 if stage < stages - 1 else 0


def hop(value, tick, count, step):
    sections, n = lax.axis_size("section"), lax.axis_size("fsdp")
    stages = sections // 2
    ticks = range(tick - tick % GROUP, tick - tick % GROUP + GROUP)
    route = []
    for s in range(sections):
        stage, core = s // 2, s % 2
        order = stage if step > 0 else stages - 1 - stage
        t = stage + step
        if 0 <= t < stages and any(0 <= k - SKEW * order < count for k in ticks):
            flip = crossed(stage, stages) ^ crossed(t, stages)
            route += [(s * n + f, (t * 2 + core) * n + (f ^ flip)) for f in range(n)]
    return lax.ppermute(value, ("section", "fsdp"), route)


GATHER = (
    ((0, 0), "zp", (-1, 0)),
    ((0, 0), "zm", (1, 0)),
    ((0, 0), "x", (0, 1)),
    ((-1, 0), "zp", (-2, 0)),
    ((1, 0), "zm", (2, 0)),
    ((-1, 0), "x", (-1, 1)),
    ((-2, 0), "zp", (-3, 0)),
    ((2, 0), "zm", (3, 0)),
    ((1, 0), "x", (1, 1)),
    ((-1, 1), "zp", (-2, 1)),
    ((1, 1), "zm", (2, 1)),
    ((-3, 0), "x", (-3, 1)),
    ((-3, 1), "zp", (-4, 1)),
    ((3, 0), "zm", (4, 0)),
    ((3, 0), "x", (3, 1)),
)
MOVE = {"zp": from_z_below, "zm": from_z_above, "x": from_x}
BACK = {"zp": from_z_above, "zm": from_z_below, "x": from_x}
KEYS = ((0, 0),) + tuple(entry[2] for entry in GATHER)


def shard_index(key):
    n = lax.axis_size("fsdp")
    me = lax.axis_index("fsdp")
    owner_z = lax.rem(me // 2 + key[0] + n // 2, n // 2)
    owner_a = lax.rem(lax.rem(me, 2) + key[1], 2)
    return owner_z * 2 + owner_a


def forward_kernel(tick, count, *refs):
    refs = list(refs)
    fresh = refs.pop(0) if tick < count else None
    incoming = refs.pop(0) if tick >= SKEW else None
    matrix, gain = refs[:2], refs[2]
    out, h_all, n_all, d_all, r_all, *turned, between = refs[-8:]
    stage, core = place()
    slot = tick - SKEW * stage
    live = (slot >= 0) & (slot < count)
    width = gain.shape[2]

    def run(first, where):
        for layer, source, target in ((0, first, between), (1, between, out)):
            h = source[...].astype(f32)
            scale = lax.rsqrt(jnp.mean(h * h, axis=-1, keepdims=True) + norm_epsilon)
            n_all[layer, where] = (h * scale * gain[layer]).astype(bf16)
            h_all[layer, where] = source[...]
            r_all[layer, where] = jnp.broadcast_to(scale, r_all.shape[2:])
            for c in range(0, width, BLOCK):
                cols = slice(c, c + BLOCK)
                p = jnp.dot(
                    n_all[layer, where], matrix[layer][:, cols], preferred_element_type=f32
                )
                gate = jax.nn.sigmoid(p)
                target[:, cols] = (source[:, cols].astype(f32) + p * gate).astype(bf16)
                d_all[layer, where, :, cols] = gate * (1.0 + p * (1.0 - gate))

    if tick < count:
        @pl.when(stage == 0)
        def _():
            run(fresh.at[core * count + tick], tick)

    if incoming is not None:
        @pl.when(live & (stage > 0))
        def _():
            run(incoming, slot)

    idle = jnp.where(slot < 0, tick, tick - count)
    pieces = 8
    rows = width // pieces

    @pl.when(jnp.logical_not(live) & (idle < pieces))
    def _():
        at = pl.multiple_of(idle * rows, rows)
        for layer in range(2):
            for c in range(0, width, BLOCK):
                cols = slice(c, c + BLOCK)
                turned[layer][cols, pl.ds(at, rows)] = matrix[layer][pl.ds(at, rows), cols].T


def forward_tick(tick, count, fresh, incoming, matrix, gain, kept):
    rows, width = fresh.shape[1:]
    operands = []
    if tick < count:
        operands.append(fresh)
    if incoming is not None:
        operands.append(incoming)
    operands += [*matrix, gain]
    first = len(kept) == 2
    shapes = [
        jax.ShapeDtypeStruct((rows, width), bf16),
        jax.ShapeDtypeStruct((2, count, rows, width), bf16),
        jax.ShapeDtypeStruct((2, count, rows, width), bf16),
        jax.ShapeDtypeStruct((2, count, rows, width), f32),
        jax.ShapeDtypeStruct((2, count, rows, 128), f32),
        jax.ShapeDtypeStruct((width, width), bf16),
        jax.ShapeDtypeStruct((width, width), bf16),
    ]
    skipped = 4 if first else 0
    aliases = {len(operands) + i: 1 + skipped + i for i in range(6 - skipped)}
    operands += list(kept)
    results = pl.pallas_call(
        functools.partial(forward_kernel, tick, count),
        in_specs=[vmem()] * len(operands),
        out_specs=[vmem()] * 7,
        out_shape=shapes,
        input_output_aliases=aliases,
        scratch_shapes=[pltpu.VMEM((rows, width), bf16)],
        compiler_params=params(4),
        name=f"forward_layer_{tick}",
    )(*operands)
    return results[0], tuple(results[1:])


def backward_kernel(tick, count, *refs):
    refs = list(refs)
    top = refs.pop(0) if tick < count else None
    incoming = refs.pop(0) if tick >= SKEW else None
    turned, (gain, h_all, d_all, r_all) = refs[:2], refs[2:6]
    out, p_all, gain_sum, between, wide = refs[-5:]
    stage, _ = place()
    stages = lax.axis_size("section") // 2
    slot = tick - SKEW * (stages - 1 - stage)
    live = (slot >= 0) & (slot < count)
    width = gain.shape[2]

    def run(first, where):
        for layer, source, target in ((1, first, between), (0, between, out)):
            p_all[layer, where] = (source[...].astype(f32) * d_all[layer, where]).astype(bf16)
            scale = r_all[layer, where][:, :1]
            dots = jnp.zeros((source.shape[0], 1), f32)
            for c in range(0, width, BLOCK):
                cols = slice(c, c + BLOCK)
                ng = jnp.dot(
                    p_all[layer, where], turned[layer][:, cols], preferred_element_type=f32
                )
                h = h_all[layer, where, :, cols].astype(f32)
                gain_rows = jnp.sum(ng * h * scale, axis=0, keepdims=True)
                before = jnp.where(where == 0, 0.0, gain_sum[layer, :, cols])
                gain_sum[layer, :, cols] = before + gain_rows
                scaled = gain[layer, :, cols] * ng
                wide[:, cols] = scaled
                dots = dots + jnp.sum(scaled * h, axis=-1, keepdims=True)
            factor = scale * scale * scale * (dots / width)
            for c in range(0, width, BLOCK):
                cols = slice(c, c + BLOCK)
                h = h_all[layer, where, :, cols].astype(f32)
                g = source[:, cols].astype(f32)
                target[:, cols] = (g + (scale * wide[:, cols] - h * factor)).astype(bf16)

    if tick < count:
        @pl.when(stage == stages - 1)
        def _():
            run(top.at[tick], tick)

    if incoming is not None:
        @pl.when(live & (stage < stages - 1))
        def _():
            run(incoming, slot)


def backward_tick(tick, count, top, incoming, turned, gain, kept, grads):
    rows, width = top.shape[1:]
    first = tick == 0
    operands = []
    if tick < count:
        operands.append(top)
    if incoming is not None:
        operands.append(incoming)
    operands += [*turned, gain, kept[0], kept[2], kept[3]]
    shapes = [
        jax.ShapeDtypeStruct((rows, width), bf16),
        jax.ShapeDtypeStruct((2, count, rows, width), bf16),
        jax.ShapeDtypeStruct((2, 1, width), f32),
    ]
    aliases = {}
    if not first:
        aliases = {len(operands) + i: 1 + i for i in range(2)}
        operands += list(grads)
    results = pl.pallas_call(
        functools.partial(backward_kernel, tick, count),
        in_specs=[vmem()] * len(operands),
        out_specs=[vmem()] * 3,
        out_shape=shapes,
        input_output_aliases=aliases,
        scratch_shapes=[pltpu.VMEM((rows, width), bf16), pltpu.VMEM((rows, width), f32)],
        compiler_params=params(4),
        name=f"backward_layer_{tick}",
    )(*operands)
    return results[0], tuple(results[1:])


def hand_over_kernel(normed, grad, gain_sum, pair, gain_other, gain_own):
    _, core = place()
    pair[0] = normed[1 - core]
    pair[1] = grad[1 - core]
    gain_other[...] = gain_sum[1 - core]
    gain_own[...] = gain_sum[core]


def hand_over(normed, grad, gain_sum):
    _, tokens, width = normed.shape
    row = jax.ShapeDtypeStruct((1, width), f32)
    return pl.pallas_call(
        hand_over_kernel,
        in_specs=[vmem()] * 3,
        out_specs=[vmem()] * 3,
        out_shape=[jax.ShapeDtypeStruct((2, tokens, width), bf16), row, row],
        compiler_params=params(4),
        name="hand_over",
    )(normed, grad, gain_sum)


def weight_kernel(normed, grad, pair, *refs):
    outs, (left_all, right_all) = refs[:-2], refs[-2:]
    _, core = place()
    tokens = normed.shape[1]
    left_all[:tokens] = normed[core]
    left_all[tokens:] = pair[0]
    right_all[:tokens] = grad[core]
    right_all[tokens:] = pair[1]
    rows = outs[0].shape[0]
    width = grad.shape[2]
    for key, out in zip(KEYS, outs):
        at = pl.multiple_of(shard_index(key) * rows, rows)
        left = left_all[:, pl.ds(at, rows)]
        for c in range(0, width, BLOCK):
            cols = slice(c, c + BLOCK)
            out[:, cols] = lax.dot_general(
                left, right_all[:, cols], (((0,), (0,)), ((), ())), preferred_element_type=f32
            ).astype(bf16)


def weight_partials(normed, grad, pair, shards):
    _, tokens, width = grad.shape
    rows = width // shards
    return pl.pallas_call(
        weight_kernel,
        in_specs=[vmem()] * 3,
        out_specs=[vmem()] * shards,
        out_shape=[jax.ShapeDtypeStruct((rows, width), bf16)] * shards,
        scratch_shapes=[pltpu.VMEM((2 * tokens, width), bf16)] * 2,
        compiler_params=params(16),
        name="weight_partials",
    )(normed, grad, pair)


def assemble_kernel(shards, *refs):
    own, other = refs[:shards], refs[shards : 2 * shards]
    smalls, (first, second, _, _, gain, sems) = refs[2 * shards : -6], refs[-6:]
    rows = own[0].shape[0]
    _, core = place()

    def lay_out(places):
        copies = []
        for i, (group, matrix) in enumerate(places):
            for j, (key, piece) in enumerate(zip(KEYS, group)):
                at = pl.multiple_of(shard_index(key) * rows, rows)
                target = matrix.at[pl.ds(at, rows)]
                copies.append(pltpu.make_async_copy(piece, target, sems.at[i, j]))
        for copy in copies:
            copy.start()
        for copy in copies:
            copy.wait()

    for i, small in enumerate(smalls):
        layer = core if i == 0 else 1 - core
        pair = small.shape[1] - 128
        for r in range(small.shape[0]):
            gain[layer, :, r * pair : (r + 1) * pair] = small[r : r + 1, :pair]

    @pl.when(core == 0)
    def _():
        lay_out(((own, first), (other, second)))

    @pl.when(core == 1)
    def _():
        lay_out(((own, second), (other, first)))


def assemble(own, other, smalls):
    shards = len(own)
    rows, width = own[0].shape
    matrix = jax.ShapeDtypeStruct((shards * rows, width), bf16)
    *matrices, gain = pl.pallas_call(
        functools.partial(assemble_kernel, shards),
        in_specs=[pl.BlockSpec(memory_space=pl.ANY)] * (2 * shards) + [vmem()] * 2,
        out_specs=[vmem()] * 5,
        out_shape=[matrix] * 4 + [jax.ShapeDtypeStruct((2, 1, width), f32)],
        scratch_shapes=[pltpu.SemaphoreType.DMA((2, shards))],
        compiler_params=params(4),
        name="assemble",
    )(*own, *other, *smalls)
    return matrices[:2], tuple(matrices[2:]), gain


def small_kernel(seq_count, *refs):
    gains, new, old, ids, advantages, *arrays = refs[:8]
    out, ids_out, adv_out, *kept, sems = refs[8:]
    copies = [pltpu.make_async_copy(a, b, sems.at[i]) for i, (a, b) in enumerate(zip(arrays, kept))]
    for copy in copies:
        copy.start()
    ids_out[...] = ids[...]
    adv_out[...] = advantages[...]
    me = lax.axis_index("fsdp")
    share = gains.shape[1]
    micro_batches = new.shape[0]
    out[...] = jnp.zeros_like(out)
    row = lax.broadcasted_iota(jnp.int32, (out.shape[0], share), 0)
    wide = jnp.where(row == me // 2, gains[...].astype(f32), 0.0)
    out[:, :share] = jnp.where(me % 2 == 0, wide, 0.0)
    out[:, share : 2 * share] = jnp.where(me % 2 == 1, wide, 0.0)
    drift = new[...] - old[...]
    lane = lax.broadcasted_iota(jnp.int32, (micro_batches, 128), 1)
    sums = jnp.zeros((micro_batches, 128), f32)
    counts = jnp.zeros((micro_batches, 128), f32)
    for k in range(seq_count):
        member = ids[...] == k
        total = jnp.sum(jnp.where(member, drift, 0.0), axis=1, keepdims=True)
        number = jnp.sum(jnp.where(member, 1.0, 0.0), axis=1, keepdims=True)
        sums = jnp.where(lane == k, total, sums)
        counts = jnp.where(lane == k, number, counts)
    out[:micro_batches, 2 * share :] = sums
    out[micro_batches : 2 * micro_batches, 2 * share :] = counts
    for copy in copies:
        copy.wait()


def small_part(gains, new, old, ids, advantages, arrays, shards):
    share = gains.shape[1]
    return pl.pallas_call(
        functools.partial(small_kernel, advantages.shape[1]),
        in_specs=[vmem()] * 5 + [pl.BlockSpec(memory_space=pl.ANY)] * len(arrays),
        out_specs=[vmem()] * (3 + len(arrays)),
        out_shape=[
            jax.ShapeDtypeStruct((shards // 2, 2 * share + 128), f32),
            jax.ShapeDtypeStruct(ids.shape, ids.dtype),
            jax.ShapeDtypeStruct(advantages.shape, f32),
        ]
        + [jax.ShapeDtypeStruct(a.shape, a.dtype) for a in arrays],
        scratch_shapes=[pltpu.SemaphoreType.DMA((len(arrays),))],
        compiler_params=params(4),
        name="small_part",
    )(gains, new, old, ids, advantages, *arrays)


def top_kernel(small, advantages, ids, direction, loss, top):
    micro_batches, seq_count = advantages.shape
    pair = small.shape[1] - 128
    sums = small[:micro_batches, pair : pair + seq_count]
    counts = small[micro_batches : 2 * micro_batches, pair : pair + seq_count]
    adv = advantages[...]
    ratio = jnp.exp(sums / counts)
    bounded = jnp.clip(ratio, 1.0 - clip_epsilon, 1.0 + clip_epsilon) * adv
    plain = ratio * adv
    least = jnp.sum(jnp.minimum(plain, bounded), axis=1, keepdims=True)
    loss[...] = -jnp.sum(least, axis=0, keepdims=True)

    stage, core = place()

    def fill(half):
        per_seq = jnp.where(plain <= bounded, -adv * ratio / counts, 0.0)
        labels = ids[...]
        coef = jnp.zeros(labels.shape, f32)
        for k in range(seq_count):
            coef = coef + jnp.where(labels == k, per_seq[:, k : k + 1], 0.0)
        n = labels.shape[1]
        rows = lax.broadcasted_iota(jnp.int32, (n, n), 0)
        same = rows == lax.broadcasted_iota(jnp.int32, (n, n), 1)
        count, size = top.shape[:2]
        for i in range(count):
            m, at = divmod((half * count + i) * size, n)
            part = slice(at, at + size)
            column = jnp.sum(jnp.where(same, coef[m : m + 1], 0.0), axis=1, keepdims=True)
            top[i] = (column[part] * direction[m, part].astype(f32)).astype(bf16)

    for half in range(2):
        pl.when((stage == lax.axis_size("section") // 2 - 1) & (core == half))(
            functools.partial(fill, half)
        )


def top_cotangent(small, advantages, ids, direction, count):
    micro_batches, rows, width = direction.shape
    return pl.pallas_call(
        top_kernel,
        in_specs=[vmem()] * 4,
        out_specs=[vmem()] * 2,
        out_shape=[
            jax.ShapeDtypeStruct((1, 1), f32),
            jax.ShapeDtypeStruct((count, micro_batches * rows // (2 * count), width), bf16),
        ],
        compiler_params=params(4),
        name="top_cotangent",
    )(small, advantages, ids, direction)


def add_kernel(*refs):
    out = refs[-1]
    acc = refs[0][...].astype(f32)
    for ref in refs[1:-1]:
        acc = acc + ref[...].astype(f32)
    out[...] = acc.astype(out.dtype)


def add(*values, kind=None):
    return pl.pallas_call(
        add_kernel,
        in_specs=[vmem()] * len(values),
        out_specs=vmem(),
        out_shape=jax.ShapeDtypeStruct(values[0].shape, kind or values[0].dtype),
        compiler_params=params(8),
        name="add",
    )(*values)


def local(
    embeddings,
    section_weights,
    section_gains,
    top_direction,
    new_logprob,
    old_logprob,
    segment_ids,
    advantages,
):
    sections = lax.axis_size("section")
    shards = lax.axis_size("fsdp")
    shard = lax.axis_index("fsdp")
    micro_batches, row_count, width = embeddings.shape
    seq_count = advantages.shape[1]
    count = COUNT
    rows = micro_batches * row_count // (2 * count)
    share = width // shards

    held = {(0, 0): section_weights[0]}
    small, ids, adv, fresh, direction, own = small_part(
        section_gains,
        new_logprob,
        old_logprob,
        segment_ids,
        advantages,
        (embeddings, top_direction, held[0, 0]),
        shards,
    )
    distance = 1
    for step in range(0, len(GATHER), 3):
        came = [MOVE[move](held[sent]) for sent, move, _ in GATHER[step : step + 3]]
        if distance < shards:
            other = from_partner(small, distance)
            came, other = lax.optimization_barrier((came, other))
            small = add(small, other)
            distance *= 2
        held.update(zip([entry[2] for entry in GATHER[step : step + 3]], came))
    fresh = fresh.reshape(2 * count, rows, width)
    other = [from_core(held[key]) for key in KEYS]
    pieces = [own] + [held[key] for key in KEYS[1:]]
    matrix, kept, gain = assemble(pieces, other, (small, from_core(small)))

    ticks = SKEW * (sections // 2 - 1) + count
    moved = {}
    for tick in range(ticks):
        state, kept = forward_tick(
            tick, count, fresh, moved.pop(tick - SKEW, None), matrix, gain, kept
        )
        if tick < ticks - SKEW:
            moved[tick] = hop(state, tick, count, 1)
        if tick == TOP_TICK:
            small, kept = lax.optimization_barrier((small, kept))
            gspo_loss, top_grad = top_cotangent(small, adv, ids, direction, count)
            gspo_loss, top_grad, kept = lax.optimization_barrier((gspo_loss, top_grad, kept))

    grads, moved = None, {}
    for tick in range(ticks):
        state, grads = backward_tick(
            tick, count, top_grad, moved.pop(tick - SKEW, None), kept[4:], gain, kept, grads
        )
        if tick < ticks - SKEW:
            moved[tick] = hop(state, tick, count, -1)
    tokens = count * rows
    normed = kept[1].reshape(2, tokens, width)
    grad = grads[0].reshape(2, tokens, width)
    pair, gain_other, gain_own = hand_over(normed, grad, grads[1])
    partials = weight_partials(normed, grad, from_core(pair), shards)
    total = dict(zip(KEYS, partials))
    gain_total = add(gain_own, from_core(gain_other), kind=bf16)
    distance = 1
    back = tuple(reversed(GATHER))
    for step in range(0, len(back), 3):
        came = {}
        for home, move, far in back[step : step + 3]:
            came.setdefault(home, []).append(BACK[move](total.pop(far)))
        if distance < shards:
            other = from_partner(gain_total, distance)
            came, other = lax.optimization_barrier((came, other))
            gain_total = add(gain_total, other, kind=f32)
            distance *= 2
        for home, values in came.items():
            total[home] = add(total[home], *values, kind=f32 if home == (0, 0) else bf16)
    gain_share = lax.dynamic_slice(gain_total, (0, shard * share), (1, share))
    return (total[0, 0][None], gain_share, gspo_loss[0, 0])


def solution(mesh):
    placed = (
        P(None, "fsdp", None),
        P("section", "fsdp", None),
        P("section", "fsdp"),
        P(None, "fsdp", None),
        P(None, "fsdp"),
        P(None, "fsdp"),
        P(None, "fsdp"),
        P(),
    )
    return jax.shard_map(
        local,
        mesh=mesh,
        in_specs=placed,
        out_specs=(P("section", "fsdp", None), P("section", "fsdp"), P()),
        check_vma=False,
    )
```

```python
import functools

import jax
import jax.numpy as jnp
from jax import lax
from jax.experimental import pallas as pl
from jax.experimental.pallas import tpu as pltpu
from jax.sharding import PartitionSpec as P

clip_epsilon = 0.2
norm_epsilon = 1e-05
COUNT = 4
SKEW = 2
GROUP = 8
TOP_TICK = 6
BLOCK = 512
f32 = jnp.float32
bf16 = jnp.bfloat16


def vmem():
    return pl.BlockSpec(memory_space=pltpu.VMEM)


def params(mib):
    return pltpu.CompilerParams(vmem_limit_bytes=mib << 20)


def from_z_below(value):
    n = lax.axis_size("fsdp")
    return lax.ppermute(value, "fsdp", [(i, (i + 2) % n) for i in range(n)])


def from_z_above(value):
    n = lax.axis_size("fsdp")
    return lax.ppermute(value, "fsdp", [(i, (i - 2) % n) for i in range(n)])


def from_x(value):
    n = lax.axis_size("fsdp")
    return lax.ppermute(value, "fsdp", [(i, i ^ 1) for i in range(n)])


def from_partner(value, distance):
    n = lax.axis_size("fsdp")
    return lax.ppermute(value, "fsdp", [(i, i ^ distance) for i in range(n)])


def from_core(value):
    n = lax.axis_size("section")
    return lax.ppermute(value, "section", [(i, i ^ 1) for i in range(n)])


def place():
    section = lax.axis_index("section")
    return section // 2, lax.rem(section, 2)


def crossed(stage, stages):
    return stage % 2 if stage < stages - 1 else 0


def hop(value, tick, count, step):
    sections, n = lax.axis_size("section"), lax.axis_size("fsdp")
    stages = sections // 2
    ticks = range(tick - tick % GROUP, tick - tick % GROUP + GROUP)
    route = []
    for s in range(sections):
        stage, core = s // 2, s % 2
        order = stage if step > 0 else stages - 1 - stage
        t = stage + step
        if 0 <= t < stages and any(0 <= k - SKEW * order < count for k in ticks):
            flip = crossed(stage, stages) ^ crossed(t, stages)
            route += [(s * n + f, (t * 2 + core) * n + (f ^ flip)) for f in range(n)]
    return lax.ppermute(value, ("section", "fsdp"), route)


GATHER = (
    ((0, 0), "zp", (-1, 0)),
    ((0, 0), "zm", (1, 0)),
    ((0, 0), "x", (0, 1)),
    ((-1, 0), "zp", (-2, 0)),
    ((1, 0), "zm", (2, 0)),
    ((-1, 0), "x", (-1, 1)),
    ((-2, 0), "zp", (-3, 0)),
    ((2, 0), "zm", (3, 0)),
    ((1, 0), "x", (1, 1)),
    ((-1, 1), "zp", (-2, 1)),
    ((1, 1), "zm", (2, 1)),
    ((-3, 0), "x", (-3, 1)),
    ((-3, 1), "zp", (-4, 1)),
    ((3, 0), "zm", (4, 0)),
    ((3, 0), "x", (3, 1)),
)
MOVE = {"zp": from_z_below, "zm": from_z_above, "x": from_x}
BACK = {"zp": from_z_above, "zm": from_z_below, "x": from_x}
EARLY = 10
KEYS = ((0, 0),) + tuple(entry[2] for entry in GATHER)


def shard_index(key):
    n = lax.axis_size("fsdp")
    me = lax.axis_index("fsdp")
    owner_z = lax.rem(me // 2 + key[0] + n // 2, n // 2)
    owner_a = lax.rem(lax.rem(me, 2) + key[1], 2)
    return owner_z * 2 + owner_a


def forward_kernel(tick, count, *refs):
    refs = list(refs)
    fresh = refs.pop(0) if tick < count else None
    incoming = refs.pop(0) if tick >= SKEW else None
    matrix, gain = refs[:2], refs[2]
    out, h_all, n_all, d_all, r_all, between = refs[-6:]
    stage, core = place()
    slot = tick - SKEW * stage
    live = (slot >= 0) & (slot < count)
    width = gain.shape[2]

    def run(first, where):
        for layer, source, target in ((0, first, between), (1, between, out)):
            h = source[...].astype(f32)
            scale = lax.rsqrt(jnp.mean(h * h, axis=-1, keepdims=True) + norm_epsilon)
            n_all[layer, where] = (h * scale * gain[layer]).astype(bf16)
            h_all[layer, where] = source[...]
            r_all[layer, where] = jnp.broadcast_to(scale, r_all.shape[2:])
            for c in range(0, width, BLOCK):
                cols = slice(c, c + BLOCK)
                p = jnp.dot(
                    n_all[layer, where], matrix[layer][:, cols], preferred_element_type=f32
                )
                gate = jax.nn.sigmoid(p)
                target[:, cols] = (source[:, cols].astype(f32) + p * gate).astype(bf16)
                d_all[layer, where, :, cols] = gate * (1.0 + p * (1.0 - gate))

    if tick < count:
        @pl.when(stage == 0)
        def _():
            run(fresh.at[core * count + tick], tick)

    if incoming is not None:
        @pl.when(live & (stage > 0))
        def _():
            run(incoming, slot)


def forward_tick(tick, count, fresh, incoming, matrix, gain, kept):
    rows, width = fresh.shape[1:]
    operands = []
    if tick < count:
        operands.append(fresh)
    if incoming is not None:
        operands.append(incoming)
    operands += [*matrix, gain]
    shapes = [
        jax.ShapeDtypeStruct((rows, width), bf16),
        jax.ShapeDtypeStruct((2, count, rows, width), bf16),
        jax.ShapeDtypeStruct((2, count, rows, width), bf16),
        jax.ShapeDtypeStruct((2, count, rows, width), f32),
        jax.ShapeDtypeStruct((2, count, rows, 128), f32),
    ]
    aliases = {len(operands) + i: 1 + i for i in range(len(kept))}
    operands += list(kept)
    results = pl.pallas_call(
        functools.partial(forward_kernel, tick, count),
        in_specs=[vmem()] * len(operands),
        out_specs=[vmem()] * 5,
        out_shape=shapes,
        input_output_aliases=aliases,
        scratch_shapes=[pltpu.VMEM((rows, width), bf16)],
        compiler_params=params(4),
        name=f"forward_layer_{tick}",
    )(*operands)
    return results[0], tuple(results[1:])


def turn_kernel(first, last, *refs):
    matrix, turned = refs[:2], refs[-2:]
    stage, _ = place()
    width = matrix[0].shape[0]

    @pl.when((stage >= first) & (stage <= last))
    def _():
        for a, b in zip(matrix, turned):
            @pl.loop(0, width // BLOCK)
            def _(i):
                at = pl.multiple_of(i * BLOCK, BLOCK)
                for c in range(0, width, BLOCK):
                    b[c : c + BLOCK, pl.ds(at, BLOCK)] = a[pl.ds(at, BLOCK), c : c + BLOCK].T


def turn(first, last, matrix, turned=()):
    operands = [*matrix, *turned]
    return pl.pallas_call(
        functools.partial(turn_kernel, first, last),
        in_specs=[vmem()] * len(operands),
        out_specs=[vmem()] * 2,
        out_shape=[jax.ShapeDtypeStruct(m.shape, m.dtype) for m in matrix],
        input_output_aliases={2 + i: i for i in range(len(turned))},
        compiler_params=params(4),
        name="turn",
    )(*operands)


def backward_kernel(tick, count, *refs):
    refs = list(refs)
    top = refs.pop(0) if tick < count else None
    incoming = refs.pop(0) if tick >= SKEW else None
    turned, (gain, h_all, d_all, r_all) = refs[:2], refs[2:6]
    out, p_all, gain_sum, between, wide = refs[-5:]
    stage, _ = place()
    stages = lax.axis_size("section") // 2
    slot = tick - SKEW * (stages - 1 - stage)
    live = (slot >= 0) & (slot < count)
    width = gain.shape[2]

    def run(first, where):
        for layer, source, target in ((1, first, between), (0, between, out)):
            p_all[layer, where] = (source[...].astype(f32) * d_all[layer, where]).astype(bf16)
            scale = r_all[layer, where][:, :1]
            dots = jnp.zeros((source.shape[0], 1), f32)
            for c in range(0, width, BLOCK):
                cols = slice(c, c + BLOCK)
                ng = jnp.dot(
                    p_all[layer, where], turned[layer][:, cols], preferred_element_type=f32
                )
                h = h_all[layer, where, :, cols].astype(f32)
                gain_rows = jnp.sum(ng * h * scale, axis=0, keepdims=True)
                before = jnp.where(where == 0, 0.0, gain_sum[layer, :, cols])
                gain_sum[layer, :, cols] = before + gain_rows
                scaled = gain[layer, :, cols] * ng
                wide[:, cols] = scaled
                dots = dots + jnp.sum(scaled * h, axis=-1, keepdims=True)
            factor = scale * scale * scale * (dots / width)
            for c in range(0, width, BLOCK):
                cols = slice(c, c + BLOCK)
                h = h_all[layer, where, :, cols].astype(f32)
                g = source[:, cols].astype(f32)
                target[:, cols] = (g + (scale * wide[:, cols] - h * factor)).astype(bf16)

    if tick < count:
        @pl.when(stage == stages - 1)
        def _():
            run(top.at[tick], tick)

    if incoming is not None:
        @pl.when(live & (stage < stages - 1))
        def _():
            run(incoming, slot)


def backward_tick(tick, count, top, incoming, turned, gain, kept, grads):
    rows, width = top.shape[1:]
    first = tick == 0
    operands = []
    if tick < count:
        operands.append(top)
    if incoming is not None:
        operands.append(incoming)
    operands += [*turned, gain, kept[0], kept[2], kept[3]]
    shapes = [
        jax.ShapeDtypeStruct((rows, width), bf16),
        jax.ShapeDtypeStruct((2, count, rows, width), bf16),
        jax.ShapeDtypeStruct((2, 1, width), f32),
    ]
    aliases = {}
    if not first:
        aliases = {len(operands) + i: 1 + i for i in range(2)}
        operands += list(grads)
    results = pl.pallas_call(
        functools.partial(backward_kernel, tick, count),
        in_specs=[vmem()] * len(operands),
        out_specs=[vmem()] * 3,
        out_shape=shapes,
        input_output_aliases=aliases,
        scratch_shapes=[pltpu.VMEM((rows, width), bf16), pltpu.VMEM((rows, width), f32)],
        compiler_params=params(4),
        name=f"backward_layer_{tick}",
    )(*operands)
    return results[0], tuple(results[1:])


def hand_over_kernel(normed, grad, gain_sum, pair, gain_other, gain_own):
    _, core = place()
    pair[0] = normed[1 - core]
    pair[1] = grad[1 - core]
    gain_other[...] = gain_sum[1 - core]
    gain_own[...] = gain_sum[core]


def hand_over(normed, grad, gain_sum):
    _, tokens, width = normed.shape
    row = jax.ShapeDtypeStruct((1, width), f32)
    return pl.pallas_call(
        hand_over_kernel,
        in_specs=[vmem()] * 3,
        out_specs=[vmem()] * 3,
        out_shape=[jax.ShapeDtypeStruct((2, tokens, width), bf16), row, row],
        compiler_params=params(4),
        name="hand_over",
    )(normed, grad, gain_sum)


def weight_kernel(normed, grad, pair, *refs):
    outs, (left_all, right_all) = refs[:-2], refs[-2:]
    _, core = place()
    tokens = normed.shape[1]
    left_all[:tokens] = normed[core]
    left_all[tokens:] = pair[0]
    right_all[:tokens] = grad[core]
    right_all[tokens:] = pair[1]
    rows = outs[0].shape[0]
    width = grad.shape[2]
    for key, out in zip(KEYS, outs):
        at = pl.multiple_of(shard_index(key) * rows, rows)
        left = left_all[:, pl.ds(at, rows)]
        for c in range(0, width, BLOCK):
            cols = slice(c, c + BLOCK)
            out[:, cols] = lax.dot_general(
                left, right_all[:, cols], (((0,), (0,)), ((), ())), preferred_element_type=f32
            ).astype(bf16)


def weight_partials(normed, grad, pair, shards):
    _, tokens, width = grad.shape
    rows = width // shards
    return pl.pallas_call(
        weight_kernel,
        in_specs=[vmem()] * 3,
        out_specs=[vmem()] * shards,
        out_shape=[jax.ShapeDtypeStruct((rows, width), bf16)] * shards,
        scratch_shapes=[pltpu.VMEM((2 * tokens, width), bf16)] * 2,
        compiler_params=params(16),
        name="weight_partials",
    )(normed, grad, pair)


def pack_kernel(*refs):
    *pieces, out, sems = refs
    copies = [
        pltpu.make_async_copy(piece, out.at[j], sems.at[j]) for j, piece in enumerate(pieces)
    ]
    for copy in copies:
        copy.start()
    for copy in copies:
        copy.wait()


def pack(pieces):
    n = len(pieces)
    return pl.pallas_call(
        pack_kernel,
        in_specs=[pl.BlockSpec(memory_space=pl.ANY)] * n,
        out_specs=vmem(),
        out_shape=jax.ShapeDtypeStruct((n, *pieces[0].shape), bf16),
        scratch_shapes=[pltpu.SemaphoreType.DMA((n,))],
        compiler_params=params(4),
        name="pack",
    )(*pieces)


def lay_out(places, sems):
    copies = []
    for keys, block, matrix in places:
        rows = block.shape[1]
        for j, key in enumerate(keys):
            at = pl.multiple_of(shard_index(key) * rows, rows)
            target = matrix.at[pl.ds(at, rows)]
            copies.append(pltpu.make_async_copy(block.at[j], target, sems.at[len(copies)]))
    for copy in copies:
        copy.start()
    for copy in copies:
        copy.wait()


def assemble_kernel(early, late, early_other, small, small_other, *refs):
    first, second, gain, sems = refs[0], refs[1], refs[-2], refs[-1]
    _, core = place()
    for layer, part in ((core, small), (1 - core, small_other)):
        pair = part.shape[1] - 128
        for r in range(part.shape[0]):
            gain[layer, :, r * pair : (r + 1) * pair] = part[r : r + 1, :pair]
    n = early.shape[0]
    for half, own, other in ((0, first, second), (1, second, first)):
        places = ((KEYS[:n], early, own), (KEYS[n:], late, own), (KEYS[:n], early_other, other))
        pl.when(core == half)(functools.partial(lay_out, places, sems))


def assemble(early, late, early_other, smalls):
    _, rows, width = early.shape
    matrix = jax.ShapeDtypeStruct((width, width), bf16)
    n = early.shape[0] * 2 + late.shape[0]
    *matrices, gain = pl.pallas_call(
        assemble_kernel,
        in_specs=[pl.BlockSpec(memory_space=pl.ANY)] * 3 + [vmem()] * 2,
        out_specs=[vmem()] * (2 + 1),
        out_shape=[matrix] * 2 + [jax.ShapeDtypeStruct((2, 1, width), f32)],
        scratch_shapes=[pltpu.SemaphoreType.DMA((n,))],
        compiler_params=params(4),
        name="assemble",
    )(early, late, early_other, *smalls)
    return matrices, gain


def complete_kernel(late_other, _, __, first, second, sems):
    _, core = place()
    keys = KEYS[len(KEYS) - late_other.shape[0] :]
    for half, other in ((0, second), (1, first)):
        pl.when(core == half)(functools.partial(lay_out, ((keys, late_other, other),), sems))


def complete(late_other, matrices):
    return pl.pallas_call(
        complete_kernel,
        in_specs=[pl.BlockSpec(memory_space=pl.ANY)] + [vmem()] * 2,
        out_specs=[vmem()] * 2,
        out_shape=[jax.ShapeDtypeStruct(m.shape, m.dtype) for m in matrices],
        input_output_aliases={1: 0, 2: 1},
        scratch_shapes=[pltpu.SemaphoreType.DMA((late_other.shape[0],))],
        compiler_params=params(4),
        name="complete",
    )(late_other, *matrices)


def small_kernel(seq_count, *refs):
    gains, new, old, ids, advantages, *arrays = refs[:8]
    out, ids_out, adv_out, *kept, sems = refs[8:]
    copies = [pltpu.make_async_copy(a, b, sems.at[i]) for i, (a, b) in enumerate(zip(arrays, kept))]
    for copy in copies:
        copy.start()
    ids_out[...] = ids[...]
    adv_out[...] = advantages[...]
    me = lax.axis_index("fsdp")
    share = gains.shape[1]
    micro_batches = new.shape[0]
    out[...] = jnp.zeros_like(out)
    row = lax.broadcasted_iota(jnp.int32, (out.shape[0], share), 0)
    wide = jnp.where(row == me // 2, gains[...].astype(f32), 0.0)
    out[:, :share] = jnp.where(me % 2 == 0, wide, 0.0)
    out[:, share : 2 * share] = jnp.where(me % 2 == 1, wide, 0.0)
    drift = new[...] - old[...]
    lane = lax.broadcasted_iota(jnp.int32, (micro_batches, 128), 1)
    sums = jnp.zeros((micro_batches, 128), f32)
    counts = jnp.zeros((micro_batches, 128), f32)
    for k in range(seq_count):
        member = ids[...] == k
        total = jnp.sum(jnp.where(member, drift, 0.0), axis=1, keepdims=True)
        number = jnp.sum(jnp.where(member, 1.0, 0.0), axis=1, keepdims=True)
        sums = jnp.where(lane == k, total, sums)
        counts = jnp.where(lane == k, number, counts)
    out[:micro_batches, 2 * share :] = sums
    out[micro_batches : 2 * micro_batches, 2 * share :] = counts
    for copy in copies:
        copy.wait()


def small_part(gains, new, old, ids, advantages, arrays, shards):
    share = gains.shape[1]
    return pl.pallas_call(
        functools.partial(small_kernel, advantages.shape[1]),
        in_specs=[vmem()] * 5 + [pl.BlockSpec(memory_space=pl.ANY)] * len(arrays),
        out_specs=[vmem()] * (3 + len(arrays)),
        out_shape=[
            jax.ShapeDtypeStruct((shards // 2, 2 * share + 128), f32),
            jax.ShapeDtypeStruct(ids.shape, ids.dtype),
            jax.ShapeDtypeStruct(advantages.shape, f32),
        ]
        + [jax.ShapeDtypeStruct(a.shape, a.dtype) for a in arrays],
        scratch_shapes=[pltpu.SemaphoreType.DMA((len(arrays),))],
        compiler_params=params(4),
        name="small_part",
    )(gains, new, old, ids, advantages, *arrays)


def top_kernel(small, advantages, ids, direction, loss, top):
    micro_batches, seq_count = advantages.shape
    pair = small.shape[1] - 128
    sums = small[:micro_batches, pair : pair + seq_count]
    counts = small[micro_batches : 2 * micro_batches, pair : pair + seq_count]
    adv = advantages[...]
    ratio = jnp.exp(sums / counts)
    bounded = jnp.clip(ratio, 1.0 - clip_epsilon, 1.0 + clip_epsilon) * adv
    plain = ratio * adv
    least = jnp.sum(jnp.minimum(plain, bounded), axis=1, keepdims=True)
    loss[...] = -jnp.sum(least, axis=0, keepdims=True)

    stage, core = place()

    def fill(half):
        per_seq = jnp.where(plain <= bounded, -adv * ratio / counts, 0.0)
        labels = ids[...]
        coef = jnp.zeros(labels.shape, f32)
        for k in range(seq_count):
            coef = coef + jnp.where(labels == k, per_seq[:, k : k + 1], 0.0)
        n = labels.shape[1]
        rows = lax.broadcasted_iota(jnp.int32, (n, n), 0)
        same = rows == lax.broadcasted_iota(jnp.int32, (n, n), 1)
        count, size = top.shape[:2]
        for i in range(count):
            m, at = divmod((half * count + i) * size, n)
            part = slice(at, at + size)
            column = jnp.sum(jnp.where(same, coef[m : m + 1], 0.0), axis=1, keepdims=True)
            top[i] = (column[part] * direction[m, part].astype(f32)).astype(bf16)

    for half in range(2):
        pl.when((stage == lax.axis_size("section") // 2 - 1) & (core == half))(
            functools.partial(fill, half)
        )


def top_cotangent(small, advantages, ids, direction, count):
    micro_batches, rows, width = direction.shape
    return pl.pallas_call(
        top_kernel,
        in_specs=[vmem()] * 4,
        out_specs=[vmem()] * 2,
        out_shape=[
            jax.ShapeDtypeStruct((1, 1), f32),
            jax.ShapeDtypeStruct((count, micro_batches * rows // (2 * count), width), bf16),
        ],
        compiler_params=params(4),
        name="top_cotangent",
    )(small, advantages, ids, direction)


def add_kernel(*refs):
    out = refs[-1]
    acc = refs[0][...].astype(f32)
    for ref in refs[1:-1]:
        acc = acc + ref[...].astype(f32)
    out[...] = acc.astype(out.dtype)


def add(*values, kind=None):
    return pl.pallas_call(
        add_kernel,
        in_specs=[vmem()] * len(values),
        out_specs=vmem(),
        out_shape=jax.ShapeDtypeStruct(values[0].shape, kind or values[0].dtype),
        compiler_params=params(8),
        name="add",
    )(*values)


def local(
    embeddings,
    section_weights,
    section_gains,
    top_direction,
    new_logprob,
    old_logprob,
    segment_ids,
    advantages,
):
    sections = lax.axis_size("section")
    shards = lax.axis_size("fsdp")
    shard = lax.axis_index("fsdp")
    micro_batches, row_count, width = embeddings.shape
    seq_count = advantages.shape[1]
    count = COUNT
    rows = micro_batches * row_count // (2 * count)
    share = width // shards

    held = {(0, 0): section_weights[0]}
    small, ids, adv, fresh, direction, own = small_part(
        section_gains,
        new_logprob,
        old_logprob,
        segment_ids,
        advantages,
        (embeddings, top_direction, held[0, 0]),
        shards,
    )
    distance = 1
    for step in range(0, len(GATHER), 3):
        came = [MOVE[move](held[sent]) for sent, move, _ in GATHER[step : step + 3]]
        if distance < shards:
            other = from_partner(small, distance)
            came, other = lax.optimization_barrier((came, other))
            small = add(small, other)
            distance *= 2
        held.update(zip([entry[2] for entry in GATHER[step : step + 3]], came))
        if len(held) == EARLY:
            early = pack([own] + [held[key] for key in KEYS[1:EARLY]])
            early_other = from_core(early)
    fresh = fresh.reshape(2 * count, rows, width)
    late = pack([held[key] for key in KEYS[EARLY:]])
    late_other = from_core(late)
    matrices, gain = assemble(early, late, early_other, (small, from_core(small)))
    matrix = complete(late_other, matrices[:2])
    kept, half = (), sections // 4

    ticks = SKEW * (sections // 2 - 1) + count
    moved = {}
    for tick in range(ticks):
        state, kept = forward_tick(
            tick, count, fresh, moved.pop(tick - SKEW, None), matrix, gain, kept
        )
        if tick < ticks - SKEW:
            moved[tick] = hop(state, tick, count, 1)
        if tick == TOP_TICK:
            small, kept = lax.optimization_barrier((small, kept))
            gspo_loss, top_grad = top_cotangent(small, adv, ids, direction, count)
            turned = turn(half, 2 * half - 1, matrix)
            gspo_loss, top_grad, turned, kept = lax.optimization_barrier(
                (gspo_loss, top_grad, turned, kept)
            )

    turned, kept = lax.optimization_barrier((turned, kept))
    turned = turn(0, half - 1, matrix, turned)

    grads, moved = None, {}
    for tick in range(ticks):
        state, grads = backward_tick(
            tick, count, top_grad, moved.pop(tick - SKEW, None), turned, gain, kept, grads
        )
        if tick < ticks - SKEW:
            moved[tick] = hop(state, tick, count, -1)
    tokens = count * rows
    normed = kept[1].reshape(2, tokens, width)
    grad = grads[0].reshape(2, tokens, width)
    pair, gain_other, gain_own = hand_over(normed, grad, grads[1])
    partials = weight_partials(normed, grad, from_core(pair), shards)
    total = dict(zip(KEYS, partials))
    gain_total = add(gain_own, from_core(gain_other), kind=bf16)
    distance = 1
    back = tuple(reversed(GATHER))
    for step in range(0, len(back), 3):
        came = {}
        for home, move, far in back[step : step + 3]:
            came.setdefault(home, []).append(BACK[move](total.pop(far)))
        if distance < shards:
            other = from_partner(gain_total, distance)
            came, other = lax.optimization_barrier((came, other))
            gain_total = add(gain_total, other, kind=f32)
            distance *= 2
        for home, values in came.items():
            total[home] = add(total[home], *values, kind=f32 if home == (0, 0) else bf16)
    gain_share = lax.dynamic_slice(gain_total, (0, shard * share), (1, share))
    return (total[0, 0][None], gain_share, gspo_loss[0, 0])


def solution(mesh):
    placed = (
        P(None, "fsdp", None),
        P("section", "fsdp", None),
        P("section", "fsdp"),
        P(None, "fsdp", None),
        P(None, "fsdp"),
        P(None, "fsdp"),
        P(None, "fsdp"),
        P(),
    )
    return jax.shard_map(
        local,
        mesh=mesh,
        in_specs=placed,
        out_specs=(P("section", "fsdp", None), P("section", "fsdp"), P()),
        check_vma=False,
    )
```

```python
import functools

import jax
import jax.numpy as jnp
from jax import lax
from jax.experimental import pallas as pl
from jax.experimental.pallas import tpu as pltpu
from jax.sharding import PartitionSpec as P

clip_epsilon = 0.2
norm_epsilon = 1e-05
COUNT = 4
SKEW = 2
GROUP = 8
TOP_TICK = 6
BLOCK = 512
f32 = jnp.float32
bf16 = jnp.bfloat16


def vmem():
    return pl.BlockSpec(memory_space=pltpu.VMEM)


def params(mib):
    return pltpu.CompilerParams(vmem_limit_bytes=mib << 20)


def from_z_below(value):
    n = lax.axis_size("fsdp")
    return lax.ppermute(value, "fsdp", [(i, (i + 2) % n) for i in range(n)])


def from_z_above(value):
    n = lax.axis_size("fsdp")
    return lax.ppermute(value, "fsdp", [(i, (i - 2) % n) for i in range(n)])


def from_x(value):
    n = lax.axis_size("fsdp")
    return lax.ppermute(value, "fsdp", [(i, i ^ 1) for i in range(n)])


def from_partner(value, distance):
    n = lax.axis_size("fsdp")
    return lax.ppermute(value, "fsdp", [(i, i ^ distance) for i in range(n)])


def from_core(value):
    n = lax.axis_size("section")
    return lax.ppermute(value, "section", [(i, i ^ 1) for i in range(n)])


def place():
    section = lax.axis_index("section")
    return section // 2, lax.rem(section, 2)


def crossed(stage, stages):
    return stage % 2 if stage < stages - 1 else 0


def hop(value, tick, count, step):
    sections, n = lax.axis_size("section"), lax.axis_size("fsdp")
    stages = sections // 2
    ticks = range(tick - tick % GROUP, tick - tick % GROUP + GROUP)
    route = []
    for s in range(sections):
        stage, core = s // 2, s % 2
        order = stage if step > 0 else stages - 1 - stage
        t = stage + step
        if 0 <= t < stages and any(0 <= k - SKEW * order < count for k in ticks):
            flip = crossed(stage, stages) ^ crossed(t, stages)
            route += [(s * n + f, (t * 2 + core) * n + (f ^ flip)) for f in range(n)]
    return lax.ppermute(value, ("section", "fsdp"), route)


GATHER = (
    ((0, 0), "zp", (-1, 0)),
    ((0, 0), "zm", (1, 0)),
    ((0, 0), "x", (0, 1)),
    ((-1, 0), "zp", (-2, 0)),
    ((1, 0), "zm", (2, 0)),
    ((-1, 0), "x", (-1, 1)),
    ((-2, 0), "zp", (-3, 0)),
    ((2, 0), "zm", (3, 0)),
    ((1, 0), "x", (1, 1)),
    ((-1, 1), "zp", (-2, 1)),
    ((1, 1), "zm", (2, 1)),
    ((-3, 0), "x", (-3, 1)),
    ((-3, 1), "zp", (-4, 1)),
    ((3, 0), "zm", (4, 0)),
    ((3, 0), "x", (3, 1)),
)
MOVE = {"zp": from_z_below, "zm": from_z_above, "x": from_x}
BACK = {"zp": from_z_above, "zm": from_z_below, "x": from_x}
EARLY = 13
KEYS = ((0, 0),) + tuple(entry[2] for entry in GATHER)


def shard_index(key):
    n = lax.axis_size("fsdp")
    me = lax.axis_index("fsdp")
    owner_z = lax.rem(me // 2 + key[0] + n // 2, n // 2)
    owner_a = lax.rem(lax.rem(me, 2) + key[1], 2)
    return owner_z * 2 + owner_a


def forward_kernel(tick, count, sends, *refs):
    refs = list(refs)
    fresh = refs.pop(0) if tick < count else None
    incoming = refs.pop(0) if tick >= SKEW else None
    matrix, gain = refs[:2], refs[2]
    h_all, n_all, d_all, r_all, between = refs[-5:]
    out = refs[-6] if sends else between
    stage, core = place()
    slot = tick - SKEW * stage
    live = (slot >= 0) & (slot < count)
    width = gain.shape[2]

    def run(first, where):
        for layer, source, target in ((0, first, between), (1, between, out)):
            h = source[...].astype(f32)
            scale = lax.rsqrt(jnp.mean(h * h, axis=-1, keepdims=True) + norm_epsilon)
            n_all[layer, where] = (h * scale * gain[layer]).astype(bf16)
            h_all[layer, where] = source[...]
            r_all[layer, where] = jnp.broadcast_to(scale, r_all.shape[2:])
            for c in range(0, width, BLOCK):
                cols = slice(c, c + BLOCK)
                p = jnp.dot(
                    n_all[layer, where], matrix[layer][:, cols], preferred_element_type=f32
                )
                gate = jax.nn.sigmoid(p)
                target[:, cols] = (source[:, cols].astype(f32) + p * gate).astype(bf16)
                d_all[layer, where, :, cols] = gate * (1.0 + p * (1.0 - gate))

    if tick < count:
        @pl.when(stage == 0)
        def _():
            run(fresh.at[core * count + tick], tick)

    if incoming is not None:
        @pl.when(live & (stage > 0))
        def _():
            run(incoming, slot)


def forward_tick(tick, count, sends, fresh, incoming, matrix, gain, kept):
    rows, width = fresh.shape[1:]
    operands = []
    if tick < count:
        operands.append(fresh)
    if incoming is not None:
        operands.append(incoming)
    operands += [*matrix, gain]
    shapes = [
        jax.ShapeDtypeStruct((rows, width), bf16),
        jax.ShapeDtypeStruct((2, count, rows, width), bf16),
        jax.ShapeDtypeStruct((2, count, rows, width), bf16),
        jax.ShapeDtypeStruct((2, count, rows, width), f32),
        jax.ShapeDtypeStruct((2, count, rows, 128), f32),
    ]
    shapes = shapes if sends else shapes[1:]
    aliases = {len(operands) + i: sends + i for i in range(len(kept))}
    operands += list(kept)
    results = pl.pallas_call(
        functools.partial(forward_kernel, tick, count, sends),
        in_specs=[vmem()] * len(operands),
        out_specs=[vmem()] * len(shapes),
        out_shape=shapes,
        input_output_aliases=aliases,
        scratch_shapes=[pltpu.VMEM((rows, width), bf16)],
        compiler_params=params(4),
        name=f"forward_layer_{tick}",
    )(*operands)
    return results[0], tuple(results[sends:])


def turn_kernel(first, last, *refs):
    matrix, turned = refs[:2], refs[-2:]
    stage, _ = place()
    width = matrix[0].shape[0]

    @pl.when((stage >= first) & (stage <= last))
    def _():
        for a, b in zip(matrix, turned):
            @pl.loop(0, width // BLOCK)
            def _(i):
                at = pl.multiple_of(i * BLOCK, BLOCK)
                for c in range(0, width, BLOCK):
                    b[c : c + BLOCK, pl.ds(at, BLOCK)] = a[pl.ds(at, BLOCK), c : c + BLOCK].T


def turn(first, last, matrix, turned=()):
    operands = [*matrix, *turned]
    return pl.pallas_call(
        functools.partial(turn_kernel, first, last),
        in_specs=[vmem()] * len(operands),
        out_specs=[vmem()] * 2,
        out_shape=[jax.ShapeDtypeStruct(m.shape, m.dtype) for m in matrix],
        input_output_aliases={2 + i: i for i in range(len(turned))},
        compiler_params=params(4),
        name="turn",
    )(*operands)


def backward_kernel(tick, count, sends, *refs):
    refs = list(refs)
    top = refs.pop(0) if tick < count else None
    incoming = refs.pop(0) if tick >= SKEW else None
    turned, (gain, h_all, d_all, r_all) = refs[:2], refs[2:6]
    p_all, gain_sum, between, wide = refs[-4:]
    out = refs[-5] if sends else between
    stage, _ = place()
    stages = lax.axis_size("section") // 2
    slot = tick - SKEW * (stages - 1 - stage)
    live = (slot >= 0) & (slot < count)
    width = gain.shape[2]

    def run(first, where):
        for layer, source, target in ((1, first, between), (0, between, out)):
            p_all[layer, where] = (source[...].astype(f32) * d_all[layer, where]).astype(bf16)
            scale = r_all[layer, where][:, :1]
            dots = jnp.zeros((source.shape[0], 1), f32)
            for c in range(0, width, BLOCK):
                cols = slice(c, c + BLOCK)
                ng = jnp.dot(
                    p_all[layer, where], turned[layer][:, cols], preferred_element_type=f32
                )
                h = h_all[layer, where, :, cols].astype(f32)
                gain_rows = jnp.sum(ng * h * scale, axis=0, keepdims=True)
                before = jnp.where(where == 0, 0.0, gain_sum[layer, :, cols])
                gain_sum[layer, :, cols] = before + gain_rows
                if layer == 0 and not sends:
                    continue
                scaled = gain[layer, :, cols] * ng
                wide[:, cols] = scaled
                dots = dots + jnp.sum(scaled * h, axis=-1, keepdims=True)
            if layer == 0 and not sends:
                continue
            factor = scale * scale * scale * (dots / width)
            for c in range(0, width, BLOCK):
                cols = slice(c, c + BLOCK)
                h = h_all[layer, where, :, cols].astype(f32)
                g = source[:, cols].astype(f32)
                target[:, cols] = (g + (scale * wide[:, cols] - h * factor)).astype(bf16)

    if tick < count:
        @pl.when(stage == stages - 1)
        def _():
            run(top.at[tick], tick)

    if incoming is not None:
        @pl.when(live & (stage < stages - 1))
        def _():
            run(incoming, slot)


def backward_tick(tick, count, sends, top, incoming, turned, gain, kept, grads):
    rows, width = top.shape[1:]
    first = tick == 0
    operands = []
    if tick < count:
        operands.append(top)
    if incoming is not None:
        operands.append(incoming)
    operands += [*turned, gain, kept[0], kept[2], kept[3]]
    shapes = [
        jax.ShapeDtypeStruct((rows, width), bf16),
        jax.ShapeDtypeStruct((2, count, rows, width), bf16),
        jax.ShapeDtypeStruct((2, 1, width), f32),
    ]
    shapes = shapes if sends else shapes[1:]
    aliases = {}
    if not first:
        aliases = {len(operands) + i: sends + i for i in range(2)}
        operands += list(grads)
    results = pl.pallas_call(
        functools.partial(backward_kernel, tick, count, sends),
        in_specs=[vmem()] * len(operands),
        out_specs=[vmem()] * len(shapes),
        out_shape=shapes,
        input_output_aliases=aliases,
        scratch_shapes=[pltpu.VMEM((rows, width), bf16), pltpu.VMEM((rows, width), f32)],
        compiler_params=params(4),
        name=f"backward_layer_{tick}",
    )(*operands)
    return results[0], tuple(results[sends:])


def hand_over_kernel(normed, grad, gain_sum, pair, gain_other, gain_own):
    _, core = place()
    pair[0] = normed[1 - core]
    pair[1] = grad[1 - core]
    gain_other[...] = gain_sum[1 - core]
    gain_own[...] = gain_sum[core]


def hand_over(normed, grad, gain_sum):
    _, tokens, width = normed.shape
    row = jax.ShapeDtypeStruct((1, width), f32)
    return pl.pallas_call(
        hand_over_kernel,
        in_specs=[vmem()] * 3,
        out_specs=[vmem()] * 3,
        out_shape=[jax.ShapeDtypeStruct((2, tokens, width), bf16), row, row],
        compiler_params=params(4),
        name="hand_over",
    )(normed, grad, gain_sum)


def weight_kernel(keys, normed, grad, pair, *refs):
    outs, (left_all, right_all) = refs[:-2], refs[-2:]
    _, core = place()
    tokens = normed.shape[1]
    left_all[:tokens] = normed[core]
    left_all[tokens:] = pair[0]
    right_all[:tokens] = grad[core]
    right_all[tokens:] = pair[1]
    rows = outs[0].shape[0]
    width = grad.shape[2]
    for key, out in zip(keys, outs):
        at = pl.multiple_of(shard_index(key) * rows, rows)
        left = left_all[:, pl.ds(at, rows)]
        for c in range(0, width, BLOCK):
            cols = slice(c, c + BLOCK)
            out[:, cols] = lax.dot_general(
                left, right_all[:, cols], (((0,), (0,)), ((), ())), preferred_element_type=f32
            ).astype(bf16)


def weight_partials(keys, normed, grad, pair, rows):
    _, tokens, width = grad.shape
    return pl.pallas_call(
        functools.partial(weight_kernel, keys),
        in_specs=[vmem()] * 3,
        out_specs=[vmem()] * len(keys),
        out_shape=[jax.ShapeDtypeStruct((rows, width), bf16)] * len(keys),
        scratch_shapes=[pltpu.VMEM((2 * tokens, width), bf16)] * 2,
        compiler_params=params(16),
        name="weight_partials",
    )(normed, grad, pair)


def pack_kernel(*refs):
    *pieces, out, sems = refs
    copies = [
        pltpu.make_async_copy(piece, out.at[j], sems.at[j]) for j, piece in enumerate(pieces)
    ]
    for copy in copies:
        copy.start()
    for copy in copies:
        copy.wait()


def pack(pieces):
    n = len(pieces)
    return pl.pallas_call(
        pack_kernel,
        in_specs=[pl.BlockSpec(memory_space=pl.ANY)] * n,
        out_specs=vmem(),
        out_shape=jax.ShapeDtypeStruct((n, *pieces[0].shape), bf16),
        scratch_shapes=[pltpu.SemaphoreType.DMA((n,))],
        compiler_params=params(4),
        name="pack",
    )(*pieces)


def lay_out(places, sems):
    copies = []
    for keys, block, matrix in places:
        rows = block.shape[1]
        for j, key in enumerate(keys):
            at = pl.multiple_of(shard_index(key) * rows, rows)
            target = matrix.at[pl.ds(at, rows)]
            copies.append(pltpu.make_async_copy(block.at[j], target, sems.at[len(copies)]))
    for copy in copies:
        copy.start()
    for copy in copies:
        copy.wait()


def assemble_kernel(early, late, early_other, first, second, sems):
    _, core = place()
    n = early.shape[0]
    for half, own, other in ((0, first, second), (1, second, first)):
        places = ((KEYS[:n], early, own), (KEYS[n:], late, own), (KEYS[:n], early_other, other))
        pl.when(core == half)(functools.partial(lay_out, places, sems))


def assemble(early, late, early_other):
    _, rows, width = early.shape
    matrix = jax.ShapeDtypeStruct((width, width), bf16)
    n = early.shape[0] * 2 + late.shape[0]
    return pl.pallas_call(
        assemble_kernel,
        in_specs=[pl.BlockSpec(memory_space=pl.ANY)] * 3,
        out_specs=[vmem()] * 2,
        out_shape=[matrix] * 2,
        scratch_shapes=[pltpu.SemaphoreType.DMA((n,))],
        compiler_params=params(4),
        name="assemble",
    )(early, late, early_other)


def complete_kernel(late_other, _, __, small, small_other, first, second, gain, sems):
    _, core = place()
    for layer, part in ((core, small), (1 - core, small_other)):
        pair = part.shape[1] - 128
        for r in range(part.shape[0]):
            gain[layer, :, r * pair : (r + 1) * pair] = part[r : r + 1, :pair]
    keys = KEYS[len(KEYS) - late_other.shape[0] :]
    for half, other in ((0, second), (1, first)):
        pl.when(core == half)(functools.partial(lay_out, ((keys, late_other, other),), sems))


def complete(late_other, matrices, smalls):
    width = matrices[0].shape[1]
    return pl.pallas_call(
        complete_kernel,
        in_specs=[pl.BlockSpec(memory_space=pl.ANY)] + [vmem()] * 4,
        out_specs=[vmem()] * 3,
        out_shape=[jax.ShapeDtypeStruct(m.shape, m.dtype) for m in matrices]
        + [jax.ShapeDtypeStruct((2, 1, width), f32)],
        input_output_aliases={1: 0, 2: 1},
        scratch_shapes=[pltpu.SemaphoreType.DMA((late_other.shape[0],))],
        compiler_params=params(4),
        name="complete",
    )(late_other, *matrices, *smalls)


def small_kernel(seq_count, *refs):
    gains, new, old, ids, advantages, *arrays = refs[:8]
    out, ids_out, adv_out, *kept, sems = refs[8:]
    copies = [pltpu.make_async_copy(a, b, sems.at[i]) for i, (a, b) in enumerate(zip(arrays, kept))]
    for copy in copies:
        copy.start()
    ids_out[...] = ids[...]
    adv_out[...] = advantages[...]
    me = lax.axis_index("fsdp")
    share = gains.shape[1]
    micro_batches = new.shape[0]
    out[...] = jnp.zeros_like(out)
    row = lax.broadcasted_iota(jnp.int32, (out.shape[0], share), 0)
    wide = jnp.where(row == me // 2, gains[...].astype(f32), 0.0)
    out[:, :share] = jnp.where(me % 2 == 0, wide, 0.0)
    out[:, share : 2 * share] = jnp.where(me % 2 == 1, wide, 0.0)
    drift = new[...] - old[...]
    lane = lax.broadcasted_iota(jnp.int32, (micro_batches, 128), 1)
    sums = jnp.zeros((micro_batches, 128), f32)
    counts = jnp.zeros((micro_batches, 128), f32)
    for k in range(seq_count):
        member = ids[...] == k
        total = jnp.sum(jnp.where(member, drift, 0.0), axis=1, keepdims=True)
        number = jnp.sum(jnp.where(member, 1.0, 0.0), axis=1, keepdims=True)
        sums = jnp.where(lane == k, total, sums)
        counts = jnp.where(lane == k, number, counts)
    out[:micro_batches, 2 * share :] = sums
    out[micro_batches : 2 * micro_batches, 2 * share :] = counts
    for copy in copies:
        copy.wait()


def small_part(gains, new, old, ids, advantages, arrays, shards):
    share = gains.shape[1]
    return pl.pallas_call(
        functools.partial(small_kernel, advantages.shape[1]),
        in_specs=[vmem()] * 5 + [pl.BlockSpec(memory_space=pl.ANY)] * len(arrays),
        out_specs=[vmem()] * (3 + len(arrays)),
        out_shape=[
            jax.ShapeDtypeStruct((shards // 2, 2 * share + 128), f32),
            jax.ShapeDtypeStruct(ids.shape, ids.dtype),
            jax.ShapeDtypeStruct(advantages.shape, f32),
        ]
        + [jax.ShapeDtypeStruct(a.shape, a.dtype) for a in arrays],
        scratch_shapes=[pltpu.SemaphoreType.DMA((len(arrays),))],
        compiler_params=params(4),
        name="small_part",
    )(gains, new, old, ids, advantages, *arrays)


def loss_kernel(small, advantages, loss, per_seq):
    micro_batches, seq_count = advantages.shape
    pair = small.shape[1] - 128
    sums = small[:micro_batches, pair : pair + seq_count]
    counts = small[micro_batches : 2 * micro_batches, pair : pair + seq_count]
    adv = advantages[...]
    ratio = jnp.exp(sums / counts)
    bounded = jnp.clip(ratio, 1.0 - clip_epsilon, 1.0 + clip_epsilon) * adv
    plain = ratio * adv
    least = jnp.sum(jnp.minimum(plain, bounded), axis=1, keepdims=True)
    loss[...] = -jnp.sum(least, axis=0, keepdims=True)
    per_seq[...] = jnp.where(plain <= bounded, -adv * ratio / counts, 0.0)


def sequence_loss(small, advantages):
    return pl.pallas_call(
        loss_kernel,
        in_specs=[vmem()] * 2,
        out_specs=[vmem()] * 2,
        out_shape=[
            jax.ShapeDtypeStruct((1, 1), f32),
            jax.ShapeDtypeStruct(advantages.shape, f32),
        ],
        compiler_params=params(4),
        name="sequence_loss",
    )(small, advantages)


def top_kernel(per_seq, ids, direction, top):
    micro_batches, seq_count = per_seq.shape
    stage, core = place()

    def fill(half):
        labels = ids[...]
        coef = jnp.zeros(labels.shape, f32)
        for k in range(seq_count):
            coef = coef + jnp.where(labels == k, per_seq[:, k : k + 1], 0.0)
        n = labels.shape[1]
        rows = lax.broadcasted_iota(jnp.int32, (n, n), 0)
        same = rows == lax.broadcasted_iota(jnp.int32, (n, n), 1)
        count, size = top.shape[:2]
        for i in range(count):
            m, at = divmod((half * count + i) * size, n)
            part = slice(at, at + size)
            column = jnp.sum(jnp.where(same, coef[m : m + 1], 0.0), axis=1, keepdims=True)
            top[i] = (column[part] * direction[m, part].astype(f32)).astype(bf16)

    for half in range(2):
        pl.when((stage == lax.axis_size("section") // 2 - 1) & (core == half))(
            functools.partial(fill, half)
        )


def top_cotangent(per_seq, ids, direction, count):
    micro_batches, rows, width = direction.shape
    shape = (count, micro_batches * rows // (2 * count), width)
    return pl.pallas_call(
        top_kernel,
        in_specs=[vmem()] * 3,
        out_specs=vmem(),
        out_shape=jax.ShapeDtypeStruct(shape, bf16),
        compiler_params=params(4),
        name="top_cotangent",
    )(per_seq, ids, direction)


def add_kernel(*refs):
    out = refs[-1]
    acc = refs[0][...].astype(f32)
    for ref in refs[1:-1]:
        acc = acc + ref[...].astype(f32)
    out[...] = acc.astype(out.dtype)


def add(*values, kind=None):
    return pl.pallas_call(
        add_kernel,
        in_specs=[vmem()] * len(values),
        out_specs=vmem(),
        out_shape=jax.ShapeDtypeStruct(values[0].shape, kind or values[0].dtype),
        compiler_params=params(8),
        name="add",
    )(*values)


def local(
    embeddings,
    section_weights,
    section_gains,
    top_direction,
    new_logprob,
    old_logprob,
    segment_ids,
    advantages,
):
    sections = lax.axis_size("section")
    shards = lax.axis_size("fsdp")
    shard = lax.axis_index("fsdp")
    micro_batches, row_count, width = embeddings.shape
    seq_count = advantages.shape[1]
    count = COUNT
    rows = micro_batches * row_count // (2 * count)
    share = width // shards

    held = {(0, 0): section_weights[0]}
    small, ids, adv, fresh, direction, own = small_part(
        section_gains,
        new_logprob,
        old_logprob,
        segment_ids,
        advantages,
        (embeddings, top_direction, held[0, 0]),
        shards,
    )
    distance = 1
    for step in range(0, len(GATHER), 3):
        came = [MOVE[move](held[sent]) for sent, move, _ in GATHER[step : step + 3]]
        if distance < shards:
            other = from_partner(small, distance)
            came, other = lax.optimization_barrier((came, other))
            small = add(small, other)
            distance *= 2
        held.update(zip([entry[2] for entry in GATHER[step : step + 3]], came))
        if len(held) == EARLY:
            early = pack([own] + [held[key] for key in KEYS[1:EARLY]])
            early_other = from_core(early)
    fresh = fresh.reshape(2 * count, rows, width)
    late = pack([held[key] for key in KEYS[EARLY:]])
    late_other = from_core(late)
    gspo_loss, per_seq = sequence_loss(small, adv)
    small, gspo_loss, per_seq = lax.optimization_barrier((small, gspo_loss, per_seq))
    small_other = from_core(small)
    matrix = assemble(early, late, early_other)
    *matrix, gain = complete(late_other, matrix, (small, small_other))
    kept, half = (), sections // 4

    ticks = SKEW * (sections // 2 - 1) + count
    moved = {}
    for tick in range(ticks):
        state, kept = forward_tick(
            tick, count, tick < ticks - SKEW, fresh, moved.pop(tick - SKEW, None), matrix, gain, kept
        )
        if tick < ticks - SKEW:
            moved[tick] = hop(state, tick, count, 1)
        if tick == TOP_TICK:
            per_seq, kept = lax.optimization_barrier((per_seq, kept))
            top_grad = top_cotangent(per_seq, ids, direction, count)
            turned = turn(half, 2 * half - 1, matrix)
            top_grad, turned, kept = lax.optimization_barrier((top_grad, turned, kept))

    turned, kept = lax.optimization_barrier((turned, kept))
    turned = turn(0, half - 1, matrix, turned)

    grads, moved = None, {}
    for tick in range(ticks):
        state, grads = backward_tick(
            tick,
            count,
            tick < ticks - SKEW,
            top_grad,
            moved.pop(tick - SKEW, None),
            turned,
            gain,
            kept,
            grads,
        )
        if tick < ticks - SKEW:
            moved[tick] = hop(state, tick, count, -1)
    tokens = count * rows
    normed = kept[1].reshape(2, tokens, width)
    grad = grads[0].reshape(2, tokens, width)
    pair, gain_other, gain_own = hand_over(normed, grad, grads[1])
    pair = from_core(pair)
    total = {}
    for keys in (KEYS[-3:], KEYS[:-3]):
        total.update(zip(keys, weight_partials(keys, normed, grad, pair, share)))
    gain_total = add(gain_own, from_core(gain_other), kind=bf16)
    distance = 1
    back = tuple(reversed(GATHER))
    for step in range(0, len(back), 3):
        came = {}
        for home, move, far in back[step : step + 3]:
            came.setdefault(home, []).append(BACK[move](total.pop(far)))
        if distance < shards:
            other = from_partner(gain_total, distance)
            came, other = lax.optimization_barrier((came, other))
            gain_total = add(gain_total, other, kind=f32)
            distance *= 2
        for home, values in came.items():
            total[home] = add(total[home], *values, kind=f32 if home == (0, 0) else bf16)
    gain_share = lax.dynamic_slice(gain_total, (0, shard * share), (1, share))
    return (total[0, 0][None], gain_share, gspo_loss[0, 0])


def solution(mesh):
    placed = (
        P(None, "fsdp", None),
        P("section", "fsdp", None),
        P("section", "fsdp"),
        P(None, "fsdp", None),
        P(None, "fsdp"),
        P(None, "fsdp"),
        P(None, "fsdp"),
        P(),
    )
    return jax.shard_map(
        local,
        mesh=mesh,
        in_specs=placed,
        out_specs=(P("section", "fsdp", None), P("section", "fsdp"), P()),
        check_vma=False,
    )
```

```python
import functools

import jax
import jax.numpy as jnp
from jax import lax
from jax.experimental import pallas as pl
from jax.experimental.pallas import tpu as pltpu
from jax.sharding import PartitionSpec as P

clip_epsilon = 0.2
norm_epsilon = 1e-05
COUNT = 4
SKEW = 2
GROUP = 8
TOP_TICK = 6
BLOCK = 512
f32 = jnp.float32
bf16 = jnp.bfloat16


def vmem():
    return pl.BlockSpec(memory_space=pltpu.VMEM)


def params(mib):
    return pltpu.CompilerParams(vmem_limit_bytes=mib << 20)


def from_z_below(value):
    n = lax.axis_size("fsdp")
    return lax.ppermute(value, "fsdp", [(i, (i + 2) % n) for i in range(n)])


def from_z_above(value):
    n = lax.axis_size("fsdp")
    return lax.ppermute(value, "fsdp", [(i, (i - 2) % n) for i in range(n)])


def from_x(value):
    n = lax.axis_size("fsdp")
    return lax.ppermute(value, "fsdp", [(i, i ^ 1) for i in range(n)])


def from_partner(value, distance):
    n = lax.axis_size("fsdp")
    return lax.ppermute(value, "fsdp", [(i, i ^ distance) for i in range(n)])


def from_core(value):
    n = lax.axis_size("section")
    return lax.ppermute(value, "section", [(i, i ^ 1) for i in range(n)])


def place():
    section = lax.axis_index("section")
    return section // 2, lax.rem(section, 2)


def crossed(stage, stages):
    return stage % 2 if stage < stages - 1 else 0


def hop(value, tick, count, step):
    sections, n = lax.axis_size("section"), lax.axis_size("fsdp")
    stages = sections // 2
    ticks = range(tick - tick % GROUP, tick - tick % GROUP + GROUP)
    route = []
    for s in range(sections):
        stage, core = s // 2, s % 2
        order = stage if step > 0 else stages - 1 - stage
        t = stage + step
        if 0 <= t < stages and any(0 <= k - SKEW * order < count for k in ticks):
            flip = crossed(stage, stages) ^ crossed(t, stages)
            route += [(s * n + f, (t * 2 + core) * n + (f ^ flip)) for f in range(n)]
    return lax.ppermute(value, ("section", "fsdp"), route)


GATHER = (
    ((0, 0), "zp", (-1, 0)),
    ((0, 0), "zm", (1, 0)),
    ((0, 0), "x", (0, 1)),
    ((-1, 0), "zp", (-2, 0)),
    ((1, 0), "zm", (2, 0)),
    ((-1, 0), "x", (-1, 1)),
    ((-2, 0), "zp", (-3, 0)),
    ((2, 0), "zm", (3, 0)),
    ((1, 0), "x", (1, 1)),
    ((-1, 1), "zp", (-2, 1)),
    ((1, 1), "zm", (2, 1)),
    ((-3, 0), "x", (-3, 1)),
    ((-3, 1), "zp", (-4, 1)),
    ((3, 0), "zm", (4, 0)),
    ((3, 0), "x", (3, 1)),
)
MOVE = {"zp": from_z_below, "zm": from_z_above, "x": from_x}
BACK = {"zp": from_z_above, "zm": from_z_below, "x": from_x}
EARLY = 13
KEYS = ((0, 0),) + tuple(entry[2] for entry in GATHER)


def shard_index(key):
    n = lax.axis_size("fsdp")
    me = lax.axis_index("fsdp")
    owner_z = lax.rem(me // 2 + key[0] + n // 2, n // 2)
    owner_a = lax.rem(lax.rem(me, 2) + key[1], 2)
    return owner_z * 2 + owner_a


def forward_kernel(tick, count, sends, *refs):
    refs = list(refs)
    fresh = refs.pop(0) if tick < count else None
    incoming = refs.pop(0) if tick >= SKEW else None
    matrix, gain = refs[:2], refs[2]
    h_all, n_all, d_all, r_all, between = refs[-5:]
    out = refs[-6] if sends else between
    stage, core = place()
    slot = tick - SKEW * stage
    live = (slot >= 0) & (slot < count)
    width = gain.shape[2]

    def run(first, where):
        for layer, source, target in ((0, first, between), (1, between, out)):
            h = source[...].astype(f32)
            scale = lax.rsqrt(jnp.mean(h * h, axis=-1, keepdims=True) + norm_epsilon)
            n_all[layer, where] = (h * scale * gain[layer]).astype(bf16)
            h_all[layer, where] = source[...]
            r_all[layer, where] = jnp.broadcast_to(scale, r_all.shape[2:])
            for c in range(0, width, BLOCK):
                cols = slice(c, c + BLOCK)
                p = jnp.dot(
                    n_all[layer, where], matrix[layer][:, cols], preferred_element_type=f32
                )
                gate = jax.nn.sigmoid(p)
                target[:, cols] = (source[:, cols].astype(f32) + p * gate).astype(bf16)
                d_all[layer, where, :, cols] = gate * (1.0 + p * (1.0 - gate))

    if tick < count:
        @pl.when(stage == 0)
        def _():
            run(fresh.at[core * count + tick], tick)

    if incoming is not None:
        @pl.when(live & (stage > 0))
        def _():
            run(incoming, slot)


def forward_tick(tick, count, sends, fresh, incoming, matrix, gain, kept):
    rows, width = fresh.shape[1:]
    operands = []
    if tick < count:
        operands.append(fresh)
    if incoming is not None:
        operands.append(incoming)
    operands += [*matrix, gain]
    shapes = [
        jax.ShapeDtypeStruct((rows, width), bf16),
        jax.ShapeDtypeStruct((2, count, rows, width), bf16),
        jax.ShapeDtypeStruct((2, count, rows, width), bf16),
        jax.ShapeDtypeStruct((2, count, rows, width), f32),
        jax.ShapeDtypeStruct((2, count, rows, 128), f32),
    ]
    shapes = shapes if sends else shapes[1:]
    aliases = {len(operands) + i: sends + i for i in range(len(kept))}
    operands += list(kept)
    results = pl.pallas_call(
        functools.partial(forward_kernel, tick, count, sends),
        in_specs=[vmem()] * len(operands),
        out_specs=[vmem()] * len(shapes),
        out_shape=shapes,
        input_output_aliases=aliases,
        scratch_shapes=[pltpu.VMEM((rows, width), bf16)],
        compiler_params=params(4),
        name=f"forward_layer_{tick}",
    )(*operands)
    return results[0], tuple(results[sends:])


def turn_kernel(first, last, *refs):
    matrix, turned = refs[:2], refs[-2:]
    stage, _ = place()
    width = matrix[0].shape[0]

    @pl.when((stage >= first) & (stage <= last))
    def _():
        for a, b in zip(matrix, turned):
            @pl.loop(0, width // BLOCK)
            def _(i):
                at = pl.multiple_of(i * BLOCK, BLOCK)
                for c in range(0, width, BLOCK):
                    b[c : c + BLOCK, pl.ds(at, BLOCK)] = a[pl.ds(at, BLOCK), c : c + BLOCK].T


def turn(first, last, matrix, turned=()):
    operands = [*matrix, *turned]
    return pl.pallas_call(
        functools.partial(turn_kernel, first, last),
        in_specs=[vmem()] * len(operands),
        out_specs=[vmem()] * 2,
        out_shape=[jax.ShapeDtypeStruct(m.shape, m.dtype) for m in matrix],
        input_output_aliases={2 + i: i for i in range(len(turned))},
        compiler_params=params(4),
        name="turn",
    )(*operands)


def backward_kernel(tick, count, sends, *refs):
    refs = list(refs)
    top = refs.pop(0) if tick < count else None
    incoming = refs.pop(0) if tick >= SKEW else None
    turned, (gain, h_all, d_all, r_all) = refs[:2], refs[2:6]
    p_all, gain_sum, between, wide = refs[-4:]
    out = refs[-5] if sends else between
    stage, _ = place()
    stages = lax.axis_size("section") // 2
    slot = tick - SKEW * (stages - 1 - stage)
    live = (slot >= 0) & (slot < count)
    width = gain.shape[2]

    def run(first, where):
        for layer, source, target in ((1, first, between), (0, between, out)):
            p_all[layer, where] = (source[...].astype(f32) * d_all[layer, where]).astype(bf16)
            scale = r_all[layer, where][:, :1]
            dots = jnp.zeros((source.shape[0], 1), f32)
            for c in range(0, width, BLOCK):
                cols = slice(c, c + BLOCK)
                ng = jnp.dot(
                    p_all[layer, where], turned[layer][:, cols], preferred_element_type=f32
                )
                h = h_all[layer, where, :, cols].astype(f32)
                gain_rows = jnp.sum(ng * h * scale, axis=0, keepdims=True)
                before = jnp.where(where == 0, 0.0, gain_sum[layer, :, cols])
                gain_sum[layer, :, cols] = before + gain_rows
                if layer == 0 and not sends:
                    continue
                scaled = gain[layer, :, cols] * ng
                wide[:, cols] = scaled
                dots = dots + jnp.sum(scaled * h, axis=-1, keepdims=True)
            if layer == 0 and not sends:
                continue
            factor = scale * scale * scale * (dots / width)
            for c in range(0, width, BLOCK):
                cols = slice(c, c + BLOCK)
                h = h_all[layer, where, :, cols].astype(f32)
                g = source[:, cols].astype(f32)
                target[:, cols] = (g + (scale * wide[:, cols] - h * factor)).astype(bf16)

    if tick < count:
        @pl.when(stage == stages - 1)
        def _():
            run(top.at[tick], tick)

    if incoming is not None:
        @pl.when(live & (stage < stages - 1))
        def _():
            run(incoming, slot)


def backward_tick(tick, count, sends, top, incoming, turned, gain, kept, grads):
    rows, width = top.shape[1:]
    first = tick == 0
    operands = []
    if tick < count:
        operands.append(top)
    if incoming is not None:
        operands.append(incoming)
    operands += [*turned, gain, kept[0], kept[2], kept[3]]
    shapes = [
        jax.ShapeDtypeStruct((rows, width), bf16),
        jax.ShapeDtypeStruct((2, count, rows, width), bf16),
        jax.ShapeDtypeStruct((2, 1, width), f32),
    ]
    shapes = shapes if sends else shapes[1:]
    aliases = {}
    if not first:
        aliases = {len(operands) + i: sends + i for i in range(2)}
        operands += list(grads)
    results = pl.pallas_call(
        functools.partial(backward_kernel, tick, count, sends),
        in_specs=[vmem()] * len(operands),
        out_specs=[vmem()] * len(shapes),
        out_shape=shapes,
        input_output_aliases=aliases,
        scratch_shapes=[pltpu.VMEM((rows, width), bf16), pltpu.VMEM((rows, width), f32)],
        compiler_params=params(4),
        name=f"backward_layer_{tick}",
    )(*operands)
    return results[0], tuple(results[sends:])


def hand_over_kernel(normed, grad, gain_sum, pair, gain_other, gain_own):
    _, core = place()
    pair[0] = normed[1 - core]
    pair[1] = grad[1 - core]
    gain_other[...] = gain_sum[1 - core]
    gain_own[...] = gain_sum[core]


def hand_over(normed, grad, gain_sum):
    _, tokens, width = normed.shape
    row = jax.ShapeDtypeStruct((1, width), f32)
    return pl.pallas_call(
        hand_over_kernel,
        in_specs=[vmem()] * 3,
        out_specs=[vmem()] * 3,
        out_shape=[jax.ShapeDtypeStruct((2, tokens, width), bf16), row, row],
        compiler_params=params(4),
        name="hand_over",
    )(normed, grad, gain_sum)


def weight_kernel(keys, normed, grad, pair, *refs):
    outs, (left_all, right_all) = refs[:-2], refs[-2:]
    _, core = place()
    tokens = normed.shape[1]
    left_all[:tokens] = normed[core]
    left_all[tokens:] = pair[0]
    right_all[:tokens] = grad[core]
    right_all[tokens:] = pair[1]
    rows = outs[0].shape[0]
    width = grad.shape[2]
    for key, out in zip(keys, outs):
        at = pl.multiple_of(shard_index(key) * rows, rows)
        left = left_all[:, pl.ds(at, rows)]
        for c in range(0, width, BLOCK):
            cols = slice(c, c + BLOCK)
            out[:, cols] = lax.dot_general(
                left, right_all[:, cols], (((0,), (0,)), ((), ())), preferred_element_type=f32
            ).astype(bf16)


def weight_partials(keys, normed, grad, pair, rows):
    _, tokens, width = grad.shape
    return pl.pallas_call(
        functools.partial(weight_kernel, keys),
        in_specs=[vmem()] * 3,
        out_specs=[vmem()] * len(keys),
        out_shape=[jax.ShapeDtypeStruct((rows, width), bf16)] * len(keys),
        scratch_shapes=[pltpu.VMEM((2 * tokens, width), bf16)] * 2,
        compiler_params=params(16),
        name="weight_partials",
    )(normed, grad, pair)


def pack_kernel(*refs):
    *pieces, out, sems = refs
    copies = [
        pltpu.make_async_copy(piece, out.at[j], sems.at[j]) for j, piece in enumerate(pieces)
    ]
    for copy in copies:
        copy.start()
    for copy in copies:
        copy.wait()


def pack(pieces):
    n = len(pieces)
    return pl.pallas_call(
        pack_kernel,
        in_specs=[pl.BlockSpec(memory_space=pl.ANY)] * n,
        out_specs=vmem(),
        out_shape=jax.ShapeDtypeStruct((n, *pieces[0].shape), bf16),
        scratch_shapes=[pltpu.SemaphoreType.DMA((n,))],
        compiler_params=params(4),
        name="pack",
    )(*pieces)


def lay_out(places, sems):
    copies = []
    for keys, block, matrix in places:
        rows = block.shape[1]
        for j, key in enumerate(keys):
            at = pl.multiple_of(shard_index(key) * rows, rows)
            target = matrix.at[pl.ds(at, rows)]
            copies.append(pltpu.make_async_copy(block.at[j], target, sems.at[len(copies)]))
    for copy in copies:
        copy.start()
    for copy in copies:
        copy.wait()


def assemble_kernel(early, late, early_other, first, second, sems):
    _, core = place()
    n = early.shape[0]
    for half, own, other in ((0, first, second), (1, second, first)):
        places = ((KEYS[:n], early, own), (KEYS[n:], late, own), (KEYS[:n], early_other, other))
        pl.when(core == half)(functools.partial(lay_out, places, sems))


def assemble(early, late, early_other):
    _, rows, width = early.shape
    matrix = jax.ShapeDtypeStruct((width, width), bf16)
    n = early.shape[0] * 2 + late.shape[0]
    return pl.pallas_call(
        assemble_kernel,
        in_specs=[pl.BlockSpec(memory_space=pl.ANY)] * 3,
        out_specs=[vmem()] * 2,
        out_shape=[matrix] * 2,
        scratch_shapes=[pltpu.SemaphoreType.DMA((n,))],
        compiler_params=params(4),
        name="assemble",
    )(early, late, early_other)


def complete_kernel(late_other, _, __, small, small_other, first, second, gain, sems):
    _, core = place()
    for layer, part in ((core, small), (1 - core, small_other)):
        pair = part.shape[1] - 128
        for r in range(part.shape[0]):
            gain[layer, :, r * pair : (r + 1) * pair] = part[r : r + 1, :pair]
    keys = KEYS[len(KEYS) - late_other.shape[0] :]
    for half, other in ((0, second), (1, first)):
        pl.when(core == half)(functools.partial(lay_out, ((keys, late_other, other),), sems))


def complete(late_other, matrices, smalls):
    width = matrices[0].shape[1]
    return pl.pallas_call(
        complete_kernel,
        in_specs=[pl.BlockSpec(memory_space=pl.ANY)] + [vmem()] * 4,
        out_specs=[vmem()] * 3,
        out_shape=[jax.ShapeDtypeStruct(m.shape, m.dtype) for m in matrices]
        + [jax.ShapeDtypeStruct((2, 1, width), f32)],
        input_output_aliases={1: 0, 2: 1},
        scratch_shapes=[pltpu.SemaphoreType.DMA((late_other.shape[0],))],
        compiler_params=params(4),
        name="complete",
    )(late_other, *matrices, *smalls)


def small_kernel(seq_count, *refs):
    gains, new, old, ids, advantages, *arrays = refs[:8]
    out, ids_out, adv_out, *kept, sems = refs[8:]
    copies = [pltpu.make_async_copy(a, b, sems.at[i]) for i, (a, b) in enumerate(zip(arrays, kept))]
    for copy in copies:
        copy.start()
    ids_out[...] = ids[...]
    adv_out[...] = advantages[...]
    me = lax.axis_index("fsdp")
    share = gains.shape[1]
    micro_batches = new.shape[0]
    out[...] = jnp.zeros_like(out)
    row = lax.broadcasted_iota(jnp.int32, (out.shape[0], share), 0)
    wide = jnp.where(row == me // 2, gains[...].astype(f32), 0.0)
    out[:, :share] = jnp.where(me % 2 == 0, wide, 0.0)
    out[:, share : 2 * share] = jnp.where(me % 2 == 1, wide, 0.0)
    drift = new[...] - old[...]
    lane = lax.broadcasted_iota(jnp.int32, (micro_batches, 128), 1)
    sums = jnp.zeros((micro_batches, 128), f32)
    counts = jnp.zeros((micro_batches, 128), f32)
    for k in range(seq_count):
        member = ids[...] == k
        total = jnp.sum(jnp.where(member, drift, 0.0), axis=1, keepdims=True)
        number = jnp.sum(jnp.where(member, 1.0, 0.0), axis=1, keepdims=True)
        sums = jnp.where(lane == k, total, sums)
        counts = jnp.where(lane == k, number, counts)
    out[:micro_batches, 2 * share :] = sums
    out[micro_batches : 2 * micro_batches, 2 * share :] = counts
    for copy in copies:
        copy.wait()


def small_part(gains, new, old, ids, advantages, arrays, shards):
    share = gains.shape[1]
    return pl.pallas_call(
        functools.partial(small_kernel, advantages.shape[1]),
        in_specs=[vmem()] * 5 + [pl.BlockSpec(memory_space=pl.ANY)] * len(arrays),
        out_specs=[vmem()] * (3 + len(arrays)),
        out_shape=[
            jax.ShapeDtypeStruct((shards // 2, 2 * share + 128), f32),
            jax.ShapeDtypeStruct(ids.shape, ids.dtype),
            jax.ShapeDtypeStruct(advantages.shape, f32),
        ]
        + [jax.ShapeDtypeStruct(a.shape, a.dtype) for a in arrays],
        scratch_shapes=[pltpu.SemaphoreType.DMA((len(arrays),))],
        compiler_params=params(4),
        name="small_part",
    )(gains, new, old, ids, advantages, *arrays)


def loss_kernel(small, advantages, loss, per_seq):
    micro_batches, seq_count = advantages.shape
    pair = small.shape[1] - 128
    sums = small[:micro_batches, pair : pair + seq_count]
    counts = small[micro_batches : 2 * micro_batches, pair : pair + seq_count]
    adv = advantages[...]
    ratio = jnp.exp(sums / counts)
    bounded = jnp.clip(ratio, 1.0 - clip_epsilon, 1.0 + clip_epsilon) * adv
    plain = ratio * adv
    least = jnp.sum(jnp.minimum(plain, bounded), axis=1, keepdims=True)
    loss[...] = -jnp.sum(least, axis=0, keepdims=True)
    per_seq[...] = jnp.where(plain <= bounded, -adv * ratio / counts, 0.0)


def sequence_loss(small, advantages):
    return pl.pallas_call(
        loss_kernel,
        in_specs=[vmem()] * 2,
        out_specs=[vmem()] * 2,
        out_shape=[
            jax.ShapeDtypeStruct((1, 1), f32),
            jax.ShapeDtypeStruct(advantages.shape, f32),
        ],
        compiler_params=params(4),
        name="sequence_loss",
    )(small, advantages)


def top_kernel(per_seq, ids, direction, top):
    micro_batches, seq_count = per_seq.shape
    stage, core = place()

    def fill(half):
        labels = ids[...]
        coef = jnp.zeros(labels.shape, f32)
        for k in range(seq_count):
            coef = coef + jnp.where(labels == k, per_seq[:, k : k + 1], 0.0)
        n = labels.shape[1]
        rows = lax.broadcasted_iota(jnp.int32, (n, n), 0)
        same = rows == lax.broadcasted_iota(jnp.int32, (n, n), 1)
        count, size = top.shape[:2]
        for i in range(count):
            m, at = divmod((half * count + i) * size, n)
            part = slice(at, at + size)
            column = jnp.sum(jnp.where(same, coef[m : m + 1], 0.0), axis=1, keepdims=True)
            top[i] = (column[part] * direction[m, part].astype(f32)).astype(bf16)

    for half in range(2):
        pl.when((stage == lax.axis_size("section") // 2 - 1) & (core == half))(
            functools.partial(fill, half)
        )


def top_cotangent(per_seq, ids, direction, count):
    micro_batches, rows, width = direction.shape
    shape = (count, micro_batches * rows // (2 * count), width)
    return pl.pallas_call(
        top_kernel,
        in_specs=[vmem()] * 3,
        out_specs=vmem(),
        out_shape=jax.ShapeDtypeStruct(shape, bf16),
        compiler_params=params(4),
        name="top_cotangent",
    )(per_seq, ids, direction)


def add_kernel(*refs):
    out = refs[-1]
    acc = refs[0][...].astype(f32)
    for ref in refs[1:-1]:
        acc = acc + ref[...].astype(f32)
    out[...] = acc.astype(out.dtype)


def add(*values, kind=None):
    return pl.pallas_call(
        add_kernel,
        in_specs=[vmem()] * len(values),
        out_specs=vmem(),
        out_shape=jax.ShapeDtypeStruct(values[0].shape, kind or values[0].dtype),
        compiler_params=params(8),
        name="add",
    )(*values)


def local(
    embeddings,
    section_weights,
    section_gains,
    top_direction,
    new_logprob,
    old_logprob,
    segment_ids,
    advantages,
):
    sections = lax.axis_size("section")
    shards = lax.axis_size("fsdp")
    shard = lax.axis_index("fsdp")
    micro_batches, row_count, width = embeddings.shape
    seq_count = advantages.shape[1]
    count = COUNT
    rows = micro_batches * row_count // (2 * count)
    share = width // shards

    held = {(0, 0): section_weights[0]}
    small, ids, adv, fresh, direction, own = small_part(
        section_gains,
        new_logprob,
        old_logprob,
        segment_ids,
        advantages,
        (embeddings, top_direction, held[0, 0]),
        shards,
    )
    distance = 1
    for step in range(0, len(GATHER), 3):
        came = [MOVE[move](held[sent]) for sent, move, _ in GATHER[step : step + 3]]
        if distance < shards:
            other = from_partner(small, distance)
            came, other = lax.optimization_barrier((came, other))
            small = add(small, other)
            distance *= 2
        held.update(zip([entry[2] for entry in GATHER[step : step + 3]], came))
        if len(held) == EARLY:
            early = pack([own] + [held[key] for key in KEYS[1:EARLY]])
            early_other = from_core(early)
    fresh = fresh.reshape(2 * count, rows, width)
    late = pack([held[key] for key in KEYS[EARLY:]])
    late_other = from_core(late)
    gspo_loss, per_seq = sequence_loss(small, adv)
    small, gspo_loss, per_seq = lax.optimization_barrier((small, gspo_loss, per_seq))
    small_other = from_core(small)
    matrix = assemble(early, late, early_other)
    *matrix, gain = complete(late_other, matrix, (small, small_other))
    kept, half = (), sections // 4

    ticks = SKEW * (sections // 2 - 1) + count
    grads, moved, moved_back = None, {}, {}
    lag = ticks - count + 1
    for tick in range(lag + ticks):
        if tick < ticks:
            sends = tick < ticks - SKEW
            state, kept = forward_tick(
                tick, count, sends, fresh, moved.pop(tick - SKEW, None), matrix, gain, kept
            )
            if sends:
                moved[tick] = hop(state, tick, count, 1)
        if tick == TOP_TICK:
            per_seq, kept = lax.optimization_barrier((per_seq, kept))
            top_grad = top_cotangent(per_seq, ids, direction, count)
            turned = turn(half, 2 * half - 1, matrix)
            top_grad, turned, kept = lax.optimization_barrier((top_grad, turned, kept))
        if tick == ticks:
            turned, kept, grads = lax.optimization_barrier((turned, kept, grads))
            turned = turn(0, half - 1, matrix, turned)
        back = tick - lag
        if back >= 0:
            sends = back < ticks - SKEW
            state, grads = backward_tick(
                back,
                count,
                sends,
                top_grad,
                moved_back.pop(back - SKEW, None),
                turned,
                gain,
                kept,
                grads,
            )
            if sends:
                moved_back[back] = hop(state, back, count, -1)
            kept, grads = lax.optimization_barrier((kept, grads))

    tokens = count * rows
    normed = kept[1].reshape(2, tokens, width)
    grad = grads[0].reshape(2, tokens, width)
    pair, gain_other, gain_own = hand_over(normed, grad, grads[1])
    pair = from_core(pair)
    total = {}
    for keys in (KEYS[-3:], KEYS[:-3]):
        total.update(zip(keys, weight_partials(keys, normed, grad, pair, share)))
    gain_total = add(gain_own, from_core(gain_other), kind=bf16)
    distance = 1
    back = tuple(reversed(GATHER))
    for step in range(0, len(back), 3):
        came = {}
        for home, move, far in back[step : step + 3]:
            came.setdefault(home, []).append(BACK[move](total.pop(far)))
        if distance < shards:
            other = from_partner(gain_total, distance)
            came, other = lax.optimization_barrier((came, other))
            gain_total = add(gain_total, other, kind=f32)
            distance *= 2
        for home, values in came.items():
            total[home] = add(total[home], *values, kind=f32 if home == (0, 0) else bf16)
    gain_share = lax.dynamic_slice(gain_total, (0, shard * share), (1, share))
    return (total[0, 0][None], gain_share, gspo_loss[0, 0])


def solution(mesh):
    placed = (
        P(None, "fsdp", None),
        P("section", "fsdp", None),
        P("section", "fsdp"),
        P(None, "fsdp", None),
        P(None, "fsdp"),
        P(None, "fsdp"),
        P(None, "fsdp"),
        P(),
    )
    return jax.shard_map(
        local,
        mesh=mesh,
        in_specs=placed,
        out_specs=(P("section", "fsdp", None), P("section", "fsdp"), P()),
        check_vma=False,
    )
```
